128 devices in a mesh: row: 4 (over z), col: 32 (over x, y, core).
Axes of the slice: x: 4, y: 4, z: 4, core: 2. Of those that a mesh axis runs over, the one named last changes fastest.
Arguments:
- momentum: float32 [2048, 53248], P('row', 'col'), may hold values from -64 to 64
- gradient: bfloat16 [2048, 53248], P('row', 'col'), may hold values from -6 to 6
- basis: float32 [53248, 1024], P('col'), may hold values from -6 to 6
Outputs:
- new_momentum: float32 [2048, 53248], P('row', 'col')
- new_basis: float32 [53248, 1024], P('col')
- update: bfloat16 [2048, 53248], P('row', 'col')
The draws below stay inside these ranges and needn't reach their ends.
All inputs are finite; a program needn't handle non-finite values.
Results may differ from the reference program's by a relative error of at most 0.001.
Values sent between devices are 32-bit elements; how exact they have to be, the bound alone decides.
A program may use at most 128 MiB of HBM per device.

```python
import math
import jax
import jax.numpy as jnp
from jax import lax

NCOL = 53248
RANK = 1024
ROWS = 2048


def draw_momentum(key, part):
    key = jax.random.fold_in(key, 11)
    key_base = jax.random.fold_in(key, 0)
    key_cols = jax.random.fold_in(key, 1)
    key_left = jax.random.fold_in(key, 3)
    key_right = jax.random.fold_in(key, 4)
    position = jnp.arange(NCOL, dtype=jnp.float32) / (NCOL - 1)
    col_factor = 0.3 * jnp.exp(jax.random.uniform(key_cols, (NCOL,), jnp.float32) * math.log(10.0)) * jnp.exp(position * math.log(3.0))
    base = jnp.clip(jax.random.normal(key_base, (ROWS, NCOL), jnp.float32), -6.0, 6.0)
    left_dirs = jnp.clip(jax.random.normal(key_left, (ROWS, 8), jnp.float32), -3.0, 3.0)
    right_dirs = jnp.clip(jax.random.normal(key_right, (8, NCOL), jnp.float32), -3.0, 3.0)
    total = base * col_factor[None, :]
    for index in range(8):
        weight_term = 0.4 * 0.6 ** index
        total = total + weight_term * left_dirs[:, index:index + 1] * right_dirs[index:index + 1, :]
    return jnp.clip(total, -64.0, 64.0).astype(jnp.float32)


def draw_basis(key, part):
    key = jax.random.fold_in(key, 23)
    result = jax.random.normal(key, (NCOL, RANK), jnp.float32)
    return jnp.clip(result, -6.0, 6.0).astype(jnp.float32)


def steps_of(own_key, dims, cuts, least, largest):
    loudness, own = 1.0, jax.random.fold_in(own_key, 6)
    for axis_at, shards_of in cuts:
        steps = jnp.exp(jax.random.uniform(jax.random.fold_in(own, axis_at), (shards_of,), jnp.float32, least / len(cuts), largest / len(cuts)))
        loudness = loudness * jnp.repeat(steps, dims[axis_at] // shards_of).reshape([-1 if axis == axis_at else 1 for axis in range(len(dims))])
    return loudness


def normal_values(own_key, shape, scale, bound, cuts=(), kind=jnp.bfloat16):
    drawn = jax.random.normal(own_key, shape, jnp.float32) * scale
    if len(cuts) > 0:
        drawn = steps_of(own_key, shape, cuts, -0.22, 0.18) * drawn
    return jnp.clip(drawn, min=-bound, max=bound).astype(kind)


def setup_inputs(seed: int = 0) -> dict:
    key_list = jax.random.split(jax.random.key(seed), 4)
    return {
        "momentum": draw_momentum(jax.random.fold_in(key_list[3], 71), 0),
        "gradient": normal_values(key_list[1], (ROWS, NCOL), 1.0, 6.0, ((0, 4), (1, 32))),
        "basis": draw_basis(jax.random.fold_in(key_list[3], 71), 0),
    }


highest = lax.Precision.HIGHEST

def reference(momentum, gradient, basis):
    buffer = momentum + gradient.astype(jnp.float32)
    projected = jnp.dot(buffer.astype(jnp.float32), basis.astype(jnp.float32), precision=highest, preferred_element_type=jnp.float32)
    gram_total = jnp.dot(projected.T.astype(jnp.float32), projected.astype(jnp.float32), precision=highest, preferred_element_type=jnp.float32)
    factor_low = jnp.linalg.cholesky(gram_total)
    identity_mat = jnp.eye(RANK, dtype=jnp.float32)
    inverse = jax.scipy.linalg.solve_triangular(factor_low, identity_mat, lower=True)
    orthonormal = jnp.dot(projected.astype(jnp.float32), inverse.T.astype(jnp.float32), precision=highest, preferred_element_type=jnp.float32)
    right_factor = lax.dot_general(buffer.astype(jnp.float32), orthonormal.astype(jnp.float32), (((0,), (0,)), ((), ())), precision=highest, preferred_element_type=jnp.float32)
    squares = lax.optimization_barrier(jnp.sum(right_factor * right_factor, axis=0))
    col_scale = jnp.sqrt(squares / NCOL + 1e-06)
    new_basis = right_factor / col_scale[None, :]
    feedback = lax.dot_general(orthonormal.astype(jnp.float32), right_factor.astype(jnp.float32), (((1,), (1,)), ((), ())), precision=highest, preferred_element_type=jnp.float32)
    new_momentum = buffer - 0.05 * feedback
    update = lax.dot_general(orthonormal.astype(jnp.float32), new_basis.astype(jnp.float32), (((1,), (1,)), ((), ())), precision=highest, preferred_element_type=jnp.float32)
    return (new_momentum, new_basis, update.astype(jnp.bfloat16))
```

```python
import functools
import jax
import jax.numpy as jnp
from jax import lax
from jax.experimental import pallas as pl
from jax.experimental.pallas import tpu as pltpu
from jax.sharding import PartitionSpec as P

highest = lax.Precision.HIGHEST
high = lax.Precision.HIGH
MESH = pl.DeviceIdType.MESH
RANK = 1024
BLK = 128
BASE = 32
SIDE = 4
HALF = RANK // 2


def dot_tn(a, b):
    return lax.dot_general(a, b, (((0,), (0,)), ((), ())), precision=highest, preferred_element_type=jnp.float32)

def dot_nn(a, b):
    return lax.dot_general(a, b, (((1,), (0,)), ((), ())), precision=highest, preferred_element_type=jnp.float32)

def lanes(col):
    return jnp.broadcast_to(col, (8, BLK))

def eliminate(tiles, off):
    lane = lax.broadcasted_iota(jnp.int32, (8, BLK), 1)
    sub = lax.broadcasted_iota(jnp.int32, (8, BLK), 0)
    n = len(tiles)
    done = []
    for g in range(n):
        first = off + 8 * g
        cols = [[lanes(tiles[t][:, first + j:first + j + 1]) for j in range(8)] for t in range(g, n)]
        inside = (lane >= first) & (lane < first + 8)
        tiles[g] = jnp.where(inside, jnp.where(lane - first == sub, 1.0, 0.0), tiles[g])
        for t in range(g + 1, n):
            tiles[t] = jnp.where(inside, 0.0, tiles[t])
        el = [[jnp.broadcast_to(cols[0][j][i:i + 1, :], (8, BLK)) if j >= i else None for j in range(8)] for i in range(8)]
        scale = jnp.zeros((8, BLK), jnp.float32)
        for i in range(8):
            rinv = 1.0 / el[i][i]
            scale = jnp.where(sub == i, el[i][i], scale)
            mult = [None] * 8
            for j in range(i + 1, 8):
                mult[j] = el[i][j] * rinv
                for l in range(j, 8):
                    el[j][l] = el[j][l] - mult[j] * el[i][l]
            row = jnp.broadcast_to(tiles[g][i:i + 1, :], (8, BLK)) * rinv
            for t in range(g, n):
                c = cols[t - g][i]
                for j in range(i + 1, 8):
                    cols[t - g][j] = cols[t - g][j] - c * mult[j]
                if t == g:
                    c = jnp.where(sub > i, c, 0.0)
                tiles[t] = tiles[t] - c * row
        done.append(tiles[g] * lax.rsqrt(scale))
    full = jnp.concatenate(done, axis=0)
    ln = lax.broadcasted_iota(jnp.int32, full.shape, 1) - off
    rw = lax.broadcasted_iota(jnp.int32, full.shape, 0)
    return jnp.where((ln > rw) & (ln < 8 * n), 0.0, full)

def invert_block(work, at):
    lane = lax.broadcasted_iota(jnp.int32, (BLK, BLK), 1)
    blk = work[pl.ds(at, BLK), pl.ds(at, BLK)]
    parts = []
    for b in range(BLK // BASE):
        lo = b * BASE
        rows = blk[0:BASE, :]
        tiles = [rows[8 * t:8 * t + 8, :] for t in range(BASE // 8)]
        s = eliminate(tiles, lo)
        parts.append(s)
        if lo + BASE < BLK:
            upd = dot_tn(s, s)
            rest = blk[BASE:, :]
            ln = lax.broadcasted_iota(jnp.int32, rest.shape, 1)
            blk = jnp.where((ln >= lo) & (ln < lo + BASE), 0.0, rest) - upd[lo + BASE:, :]
    f = jnp.concatenate(parts, axis=0)
    row = lax.broadcasted_iota(jnp.int32, (BLK, BLK), 0)
    return jnp.where(row >= lane, f, 0.0)


def inverse_kernel(proj_ref, out_ref, work, panel):
    wide = 2 * BLK
    for i in range(RANK // wide):
        lo = i * wide
        work[lo:lo + wide, lo:] = dot_tn(proj_ref[:, lo:lo + wide], proj_ref[:, lo:])
    out_ref[...] = jnp.zeros_like(out_ref)
    nb = RANK // BLK
    for j in range(nb):
        at = j * BLK
        f = invert_block(work, at)
        if at:
            panel[:, 0:at] = dot_nn(f, work[at:at + BLK, 0:at])
        if j + 1 < nb:
            panel[:, at + BLK:] = dot_nn(f, work[at:at + BLK, at + BLK:])
        panel[:, at:at + BLK] = f
        out_ref[at:at + BLK, 0:at + BLK] = panel[:, 0:at + BLK]
        for i in range(j + 1, nb):
            lo = i * BLK
            left = panel[:, lo:lo + BLK]
            if at:
                work[lo:lo + BLK, 0:at] -= dot_tn(left, panel[:, 0:at])
            work[lo:lo + BLK, at:at + BLK] = -dot_tn(left, f)
            work[lo:lo + BLK, lo:] -= dot_tn(left, panel[:, lo:])


def inverse_factor(projected):
    return pl.pallas_call(
        inverse_kernel,
        out_shape=jax.ShapeDtypeStruct((RANK, RANK), jnp.float32),
        in_specs=[pl.BlockSpec(memory_space=pltpu.VMEM)],
        out_specs=pl.BlockSpec(memory_space=pltpu.VMEM),
        scratch_shapes=[pltpu.VMEM((RANK, RANK), jnp.float32), pltpu.VMEM((BLK, RANK), jnp.float32)],
        compiler_params=pltpu.CompilerParams(vmem_limit_bytes=48 * 2**20),
        cost_estimate=pl.CostEstimate(flops=60 * 10**9, bytes_accessed=12 * 2**20, transcendentals=0),
        name="inverse_factor",
    )(projected)


def place():
    col = lax.axis_index("col")
    return lax.axis_index("row"), col // (2 * SIDE), lax.rem(col // 2, SIDE), lax.rem(col, 2)


def ring(at, step):
    return lax.rem(at + step, SIDE)


def device(z, x, y, core):
    return (z, (x * SIDE + y) * 2 + core)


def greet(peers):
    barrier = pltpu.get_barrier_semaphore()
    for peer in peers:
        pl.semaphore_signal(barrier, inc=1, device_id=peer, device_id_type=MESH)
    pl.semaphore_wait(barrier, len(peers))


def remote(src, dst, send, recv, to):
    return pltpu.make_async_remote_copy(
        src_ref=src, dst_ref=dst, send_sem=send, recv_sem=recv, device_id=to, device_id_type=MESH
    )


def gather_kernel(part_ref, out_ref, paired, total, slots1, sums, slots2, *sems):
    pair_s, pair_r, rs1_s, rs1_r, rs2_s, rs2_r, z_s, z_r, ag1_s, ag1_r, near_s, near_r, far_s, far_r, fwd_s, fwd_r = sems
    z, x, y, core = place()
    lanes_of = (pl.ds(0, HALF), pl.ds(HALF, HALF))
    outer = (x, y)
    inner = (y, x)

    def outer_peer(h, step):
        return device(z, ring(x, step), y, core) if h == 0 else device(z, x, ring(y, step), core)

    def inner_peer(h, step):
        return outer_peer(1 - h, step)

    twin = device(z, x, y, 1 - core)
    sides = [outer_peer(h, step) for h in range(2) for step in range(1, SIDE)]
    stack = [device(ring(z, step), x, y, core) for step in range(1, SIDE)]
    greet([twin] + sides + stack)
    sent = []

    def push(copy):
        copy.start()
        sent.append(copy)

    swap = remote(part_ref.at[1 - core], paired, pair_s, pair_r, twin)
    push(swap)
    swap.wait_recv()
    total[...] = part_ref[core] + paired[...]
    first = [[None] * 3, [None] * 3]
    for h in range(2):
        for step in (2, 1, 3):
            copy = remote(
                total.at[ring(outer[h], step), :, lanes_of[h]], slots1.at[h, step - 1],
                rs1_s.at[h, step - 1], rs1_r.at[h, step - 1], outer_peer(h, step),
            )
            push(copy)
            first[h][step - 1] = copy
    second = [[None] * 3, [None] * 3]
    for h in range(2):
        for copy in first[h]:
            copy.wait_recv()
        mine = total[outer[h], :, h * HALF:(h + 1) * HALF]
        summed = mine + slots1[h, 0] + slots1[h, 1] + slots1[h, 2]
        sums[h] = summed.reshape(SIDE, 16, HALF)
        for step in (2, 1, 3):
            copy = remote(
                sums.at[h, ring(inner[h], step)], slots2.at[h, step - 1],
                rs2_s.at[h, step - 1], rs2_r.at[h, step - 1], inner_peer(h, step),
            )
            push(copy)
            second[h][step - 1] = copy

    def own(h, slab):
        return out_ref.at[slab, core, outer[h], inner[h], :, lanes_of[h]]

    up = [[None] * 3, [None] * 3]
    for h in range(2):
        for copy in second[h]:
            copy.wait_recv()
        done = sums[h, inner[h]] + slots2[h, 0] + slots2[h, 1] + slots2[h, 2]
        out_ref[z, core, outer[h], inner[h], :, h * HALF:(h + 1) * HALF] = done
        for step in (2, 1, 3):
            copy = remote(own(h, z), own(h, z), z_s.at[h, step - 1], z_r.at[h, step - 1], stack[step - 1])
            push(copy)
            up[h][step - 1] = copy

    def strip(h, place_in):
        return out_ref.at[:, core, outer[h], place_in, :, lanes_of[h]]

    back = [[None] * 3, [None] * 3]
    for h in range(2):
        for copy in up[h]:
            copy.wait_recv()
        for step in (2, 1, 3):
            copy = remote(
                strip(h, inner[h]), strip(h, inner[h]), ag1_s.at[h, step - 1], ag1_r.at[h, step - 1], inner_peer(h, step)
            )
            push(copy)
            back[h][step - 1] = copy

    def block(h, slab, group):
        return out_ref.at[slab, core, group, :, :, lanes_of[h]]

    def give(h, group, at):
        ref = out_ref.at[:, core, group, :, :, lanes_of[h]]
        copy = remote(ref, ref, fwd_s.at[h, at], fwd_r.at[h, at], twin)
        push(copy)
        return copy

    order = ((0, 1, 2, 3), (2, 3, 0, 1))
    near = {}
    for h in range(2):
        for copy in back[h]:
            copy.wait_recv()
        for at in range(SIDE):
            for side in range(2):
                slab = order[side][at]
                ref = block(h, slab, outer[h])
                copy = remote(
                    ref, ref, near_s.at[h, side, slab], near_r.at[h, side, slab], outer_peer(h, 1 if side == 0 else SIDE - 1)
                )
                push(copy)
                near[h, side, slab] = copy
    got = []
    for h in range(2):
        got.append(give(h, outer[h], 0))
    far = {}
    for at in range(2):
        for h in range(2):
            for side in range(2):
                slab = order[side][at]
                near[h, side, slab].wait_recv()
                ref = block(h, slab, ring(outer[h], SIDE - 1 if side == 0 else 1))
                copy = remote(
                    ref, ref, far_s.at[h, slab], far_r.at[h, slab], outer_peer(h, 1 if side == 0 else SIDE - 1)
                )
                push(copy)
                far[h, slab] = copy
    for h in range(2):
        for side in range(2):
            for at in range(2, SIDE):
                near[h, side, order[side][at]].wait_recv()
            got.append(give(h, ring(outer[h], SIDE - 1 if side == 0 else 1), 1 + side))
    for h in range(2):
        for slab in range(SIDE):
            far[h, slab].wait_recv()
        got.append(give(h, ring(outer[h], 2), 3))
    for copy in got:
        copy.wait_recv()
    for copy in sent:
        copy.wait_send()


def gather_projected(part):
    rows = part.shape[0]
    sem = pltpu.SemaphoreType.DMA
    six = sem((2, 3))
    out = pl.pallas_call(
        gather_kernel,
        out_shape=jax.ShapeDtypeStruct((SIDE, 2, SIDE, SIDE, 16, RANK), jnp.float32),
        in_specs=[pl.BlockSpec(memory_space=pltpu.VMEM)],
        out_specs=pl.BlockSpec(memory_space=pltpu.VMEM),
        scratch_shapes=[
            pltpu.VMEM((SIDE, 64, RANK), jnp.float32),
            pltpu.VMEM((SIDE, 64, RANK), jnp.float32),
            pltpu.VMEM((2, 3, 64, HALF), jnp.float32),
            pltpu.VMEM((2, SIDE, 16, HALF), jnp.float32),
            pltpu.VMEM((2, 3, 16, HALF), jnp.float32),
            sem(()), sem(()), six, six, six, six, six, six, six, six,
            sem((2, 2, SIDE)), sem((2, 2, SIDE)), sem((2, SIDE)), sem((2, SIDE)), sem((2, SIDE)), sem((2, SIDE)),
        ],
        compiler_params=pltpu.CompilerParams(collective_id=0, has_side_effects=True, vmem_limit_bytes=32 * 2**20),
        cost_estimate=pl.CostEstimate(flops=10**6, bytes_accessed=12 * 2**20, transcendentals=0),
        name="gather_projected",
    )(part.reshape(2, SIDE, 64, RANK))
    return out.reshape(SIDE * rows, RANK)


def norm_kernel(part_ref, out_ref, held, slots, pair_s, pair_r, one_s, one_r, two_s, two_r):
    z, x, y, core = place()
    twin = device(z, x, y, 1 - core)
    along_x = [device(z, ring(x, step), y, core) for step in range(1, SIDE)]
    along_y = [device(z, x, ring(y, step), core) for step in range(1, SIDE)]
    greet([twin] + along_x + along_y)
    swap = remote(part_ref, slots.at[0], pair_s, pair_r, twin)
    swap.start()
    swap.wait()
    held[0] = part_ref[...] + slots[0]
    for turn, (peers, send, recv) in enumerate(((along_x, one_s, one_r), (along_y, two_s, two_r))):
        copies = []
        for step in range(3):
            copy = remote(held.at[turn], slots.at[1 + 3 * turn + step], send.at[step], recv.at[step], peers[step])
            copy.start()
            copies.append(copy)
        for copy in copies:
            copy.wait()
        summed = held[turn] + slots[1 + 3 * turn] + slots[2 + 3 * turn] + slots[3 + 3 * turn]
        if turn == 0:
            held[1] = summed
        else:
            out_ref[...] = summed


def sum_norms(part):
    sem = pltpu.SemaphoreType.DMA
    tile = (8, BLK)
    out = pl.pallas_call(
        norm_kernel,
        out_shape=jax.ShapeDtypeStruct(tile, jnp.float32),
        in_specs=[pl.BlockSpec(memory_space=pltpu.VMEM)],
        out_specs=pl.BlockSpec(memory_space=pltpu.VMEM),
        scratch_shapes=[
            pltpu.VMEM((2,) + tile, jnp.float32),
            pltpu.VMEM((7,) + tile, jnp.float32),
            sem(()), sem(()), sem((3,)), sem((3,)), sem((3,)), sem((3,)),
        ],
        compiler_params=pltpu.CompilerParams(collective_id=1, has_side_effects=True),
        name="sum_norms",
    )(part.reshape(tile))
    return out.reshape(RANK)


def dot(a, b, contract, precision):
    return lax.dot_general(a, b, (contract, ((), ())), precision=precision, preferred_element_type=jnp.float32)


def body(momentum, gradient, basis):
    rows = momentum.shape[0]
    total_cols = basis.shape[0] * lax.axis_size("col")
    buffer = momentum + gradient.astype(jnp.float32)
    cuts = (0, 384, 768, 1152, 1664)
    gathered = [
        lax.all_gather(buffer[:, lo:hi], "row", axis=0, tiled=True) for lo, hi in zip(cuts[:-1], cuts[1:])
    ]
    local_proj = dot(buffer, basis, ((1,), (0,)), high)
    projected = gather_projected(local_proj)
    inverse = inverse_factor(projected)
    orthonormal = dot(projected, inverse, ((1,), (1,)), high)
    own_rows = lax.dynamic_slice_in_dim(orthonormal, lax.axis_index("row") * rows, rows, 0)
    right_factor = jnp.concatenate([dot(piece, orthonormal, ((0,), (0,)), high) for piece in gathered], axis=0)
    squares = sum_norms(jnp.sum(right_factor * right_factor, axis=0))
    col_scale = jnp.sqrt(squares / total_cols + 1e-06)
    new_basis = right_factor / col_scale[None, :]
    feedback = dot(own_rows, right_factor, ((1,), (1,)), lax.Precision.DEFAULT)
    new_momentum = buffer - 0.05 * feedback
    update = dot(own_rows, new_basis, ((1,), (1,)), high)
    return (new_momentum, new_basis, update.astype(jnp.bfloat16))


def solution(mesh):
    in_specs = (P("row", "col"), P("row", "col"), P("col", None))
    out_specs = (P("row", "col"), P("col", None), P("row", "col"))
    return jax.shard_map(body, mesh=mesh, in_specs=in_specs, out_specs=out_specs, check_vma=False)
```

```python
import functools
import jax
import jax.numpy as jnp
from jax import lax
from jax.experimental import pallas as pl
from jax.experimental.pallas import tpu as pltpu
from jax.sharding import PartitionSpec as P

highest = lax.Precision.HIGHEST
high = lax.Precision.HIGH
MESH = pl.DeviceIdType.MESH
RANK = 1024
BLK = 128
BASE = 32
SIDE = 4
HALF = RANK // 2


def dot_tn(a, b):
    return lax.dot_general(a, b, (((0,), (0,)), ((), ())), precision=highest, preferred_element_type=jnp.float32)

def dot_nn(a, b):
    return lax.dot_general(a, b, (((1,), (0,)), ((), ())), precision=highest, preferred_element_type=jnp.float32)

def lanes(col):
    return jnp.broadcast_to(col, (8, BLK))

def eliminate(tiles, off):
    lane = lax.broadcasted_iota(jnp.int32, (8, BLK), 1)
    sub = lax.broadcasted_iota(jnp.int32, (8, BLK), 0)
    n = len(tiles)
    done = []
    for g in range(n):
        first = off + 8 * g
        cols = [[lanes(tiles[t][:, first + j:first + j + 1]) for j in range(8)] for t in range(g, n)]
        inside = (lane >= first) & (lane < first + 8)
        tiles[g] = jnp.where(inside, jnp.where(lane - first == sub, 1.0, 0.0), tiles[g])
        for t in range(g + 1, n):
            tiles[t] = jnp.where(inside, 0.0, tiles[t])
        el = [[jnp.broadcast_to(cols[0][j][i:i + 1, :], (8, BLK)) if j >= i else None for j in range(8)] for i in range(8)]
        scale = jnp.zeros((8, BLK), jnp.float32)
        for i in range(8):
            rinv = 1.0 / el[i][i]
            scale = jnp.where(sub == i, el[i][i], scale)
            mult = [None] * 8
            for j in range(i + 1, 8):
                mult[j] = el[i][j] * rinv
                for l in range(j, 8):
                    el[j][l] = el[j][l] - mult[j] * el[i][l]
            row = jnp.broadcast_to(tiles[g][i:i + 1, :], (8, BLK)) * rinv
            for t in range(g, n):
                c = cols[t - g][i]
                for j in range(i + 1, 8):
                    cols[t - g][j] = cols[t - g][j] - c * mult[j]
                if t == g:
                    c = jnp.where(sub > i, c, 0.0)
                tiles[t] = tiles[t] - c * row
        done.append(tiles[g] * lax.rsqrt(scale))
    full = jnp.concatenate(done, axis=0)
    ln = lax.broadcasted_iota(jnp.int32, full.shape, 1) - off
    rw = lax.broadcasted_iota(jnp.int32, full.shape, 0)
    return jnp.where((ln > rw) & (ln < 8 * n), 0.0, full)

def invert_block(work, at):
    lane = lax.broadcasted_iota(jnp.int32, (BLK, BLK), 1)
    blk = work[pl.ds(at, BLK), pl.ds(at, BLK)]
    parts = []
    for b in range(BLK // BASE):
        lo = b * BASE
        rows = blk[0:BASE, :]
        tiles = [rows[8 * t:8 * t + 8, :] for t in range(BASE // 8)]
        s = eliminate(tiles, lo)
        parts.append(s)
        if lo + BASE < BLK:
            upd = dot_tn(s, s)
            rest = blk[BASE:, :]
            ln = lax.broadcasted_iota(jnp.int32, rest.shape, 1)
            blk = jnp.where((ln >= lo) & (ln < lo + BASE), 0.0, rest) - upd[lo + BASE:, :]
    f = jnp.concatenate(parts, axis=0)
    row = lax.broadcasted_iota(jnp.int32, (BLK, BLK), 0)
    return jnp.where(row >= lane, f, 0.0)


def inverse_kernel(proj_ref, out_ref, work, panel):
    wide = 2 * BLK
    for i in range(RANK // wide):
        lo = i * wide
        work[lo:lo + wide, lo:] = dot_tn(proj_ref[:, lo:lo + wide], proj_ref[:, lo:])
    out_ref[...] = jnp.zeros_like(out_ref)
    nb = RANK // BLK
    for j in range(nb):
        at = j * BLK
        f = invert_block(work, at)
        if at:
            panel[:, 0:at] = dot_nn(f, work[at:at + BLK, 0:at])
        if j + 1 < nb:
            panel[:, at + BLK:] = dot_nn(f, work[at:at + BLK, at + BLK:])
        panel[:, at:at + BLK] = f
        out_ref[at:at + BLK, 0:at + BLK] = panel[:, 0:at + BLK]
        for i in range(j + 1, nb):
            lo = i * BLK
            left = panel[:, lo:lo + BLK]
            if at:
                work[lo:lo + BLK, 0:at] -= dot_tn(left, panel[:, 0:at])
            work[lo:lo + BLK, at:at + BLK] = -dot_tn(left, f)
            work[lo:lo + BLK, lo:] -= dot_tn(left, panel[:, lo:])


def inverse_factor(projected):
    return pl.pallas_call(
        inverse_kernel,
        out_shape=jax.ShapeDtypeStruct((RANK, RANK), jnp.float32),
        in_specs=[pl.BlockSpec(memory_space=pltpu.VMEM)],
        out_specs=pl.BlockSpec(memory_space=pltpu.VMEM),
        scratch_shapes=[pltpu.VMEM((RANK, RANK), jnp.float32), pltpu.VMEM((BLK, RANK), jnp.float32)],
        compiler_params=pltpu.CompilerParams(vmem_limit_bytes=28 * 2**20),
        cost_estimate=pl.CostEstimate(flops=60 * 10**9, bytes_accessed=12 * 2**20, transcendentals=0),
        name="inverse_factor",
    )(projected)


def place():
    col = lax.axis_index("col")
    return lax.axis_index("row"), col // (2 * SIDE), lax.rem(col // 2, SIDE), lax.rem(col, 2)


def ring(at, step):
    return lax.rem(at + step, SIDE)


def device(z, x, y, core):
    return (z, (x * SIDE + y) * 2 + core)


def greet(peers):
    barrier = pltpu.get_barrier_semaphore()
    for peer in peers:
        pl.semaphore_signal(barrier, inc=1, device_id=peer, device_id_type=MESH)
    pl.semaphore_wait(barrier, len(peers))


def remote(src, dst, send, recv, to):
    return pltpu.make_async_remote_copy(
        src_ref=src, dst_ref=dst, send_sem=send, recv_sem=recv, device_id=to, device_id_type=MESH
    )


def gather_kernel(part_ref, turned_ref, out_ref, rows_ref, paired, total, far, near, sums, slots2, relay, *sems):
    (pair_s, pair_r, far_s, far_r, near_s, near_r, rs2_s, rs2_r, z_s, z_r, in_s, in_r, out_s, out_r,
     fwd_s, fwd_r, hop_s, hop_r, pass_s, pass_r, give_s, give_r) = sems
    z, x, y, core = place()
    lanes_of = (pl.ds(0, HALF), pl.ds(HALF, HALF))
    outer = (x, y)
    inner = (y, x)

    def outer_peer(h, step):
        return device(z, ring(x, step), y, core) if h == 0 else device(z, x, ring(y, step), core)

    def inner_peer(h, step):
        return outer_peer(1 - h, step)

    turn = (1, SIDE - 1)
    twin = device(z, x, y, 1 - core)
    sides = [outer_peer(h, step) for h in range(2) for step in range(1, SIDE)]
    stack = [device(ring(z, step), x, y, core) for step in range(1, SIDE)]
    greet([twin] + sides + stack)
    sent = []

    def push(*args):
        copy = remote(*args)
        copy.start()
        sent.append(copy)
        return copy

    swap = push(part_ref.at[1 - core], paired, pair_s, pair_r, twin)

    share, slab_rows = rows_ref.shape[0], turned_ref.shape[1]
    part = share // 2

    def columns(to, side):
        return turned_ref.at[pl.ds(pl.multiple_of(to * share + side * part, 8), part), :]

    hops = []
    for side in range(2):
        hops.append(
            push(columns(ring(z, 2), side), relay.at[side], hop_s.at[side, 0], hop_r.at[side, 0], stack[turn[side] - 1])
        )

    def landing(slab, side):
        return rows_ref.at[pl.ds(side * part, part), pl.ds(pl.multiple_of(slab * slab_rows, 128), slab_rows)]

    swap.wait_recv()
    total[...] = part_ref[core] + paired[...]
    half_rows = (pl.ds(0, 32), pl.ds(32, 32))
    first, early = {}, {}
    for h in range(2):
        for side in range(2):
            first[h, side] = push(
                total.at[ring(outer[h], 2), half_rows[side], lanes_of[h]], far.at[h, side],
                far_s.at[h, side], far_r.at[h, side], outer_peer(h, turn[side]),
            )
        for side in range(2):
            early[h, side] = push(
                total.at[ring(outer[h], turn[side]), half_rows[1 - side], lanes_of[h]], near.at[h, side, half_rows[1 - side]],
                near_s.at[h, side, 0], near_r.at[h, side, 0], outer_peer(h, turn[side]),
            )
    late = {}
    for h in range(2):
        for side in range(2):
            first[h, side].wait_recv()
            block = ring(outer[h], turn[side])
            total[block, 32 * side:32 * side + 32, h * HALF:(h + 1) * HALF] += far[h, side]
            late[h, side] = push(
                total.at[block, half_rows[side], lanes_of[h]], near.at[h, side, half_rows[side]],
                near_s.at[h, side, 1], near_r.at[h, side, 1], outer_peer(h, turn[side]),
            )
    second = [[None] * 3, [None] * 3]
    for h in range(2):
        for side in range(2):
            early[h, side].wait_recv()
            late[h, side].wait_recv()
        summed = total[outer[h], :, h * HALF:(h + 1) * HALF] + near[h, 0] + near[h, 1]
        sums[h] = summed.reshape(SIDE, 16, HALF)
        for step in (2, 1, 3):
            second[h][step - 1] = push(
                sums.at[h, ring(inner[h], step)], slots2.at[h, step - 1],
                rs2_s.at[h, step - 1], rs2_r.at[h, step - 1], inner_peer(h, step),
            )

    up = [[None] * 3, [None] * 3]
    for h in range(2):
        for copy in second[h]:
            copy.wait_recv()
        done = sums[h, inner[h]] + slots2[h, 0] + slots2[h, 1] + slots2[h, 2]
        out_ref[z, core, outer[h], inner[h], :, h * HALF:(h + 1) * HALF] = done
        own = out_ref.at[z, core, outer[h], inner[h], :, lanes_of[h]]
        for step in (2, 1, 3):
            up[h][step - 1] = push(own, own, z_s.at[h, step - 1], z_r.at[h, step - 1], stack[step - 1])

    rows_ref[:, pl.ds(pl.multiple_of(z * slab_rows, 128), slab_rows)] = turned_ref[
        pl.ds(pl.multiple_of(z * share, 8), share), :
    ]

    def spread(h, at, peer, ref_of, cuts, send, recv, fwd_send, fwd_recv):
        count = len(cuts)
        order = (list(range(count)), list(range(count // 2, count)) + list(range(count // 2)))
        copies, passed = {}, {}
        for k in range(count):
            for side in range(2):
                cut = order[side][k]
                ref = ref_of(cuts[cut], at)
                copies[side, cut] = push(ref, ref, send.at[h, side, cut], recv.at[h, side, cut], peer(h, turn[side]))

        def relay_on(k):
            for side in range(2):
                cut = order[side][k]
                copies[side, cut].wait_recv()
                ref = ref_of(cuts[cut], ring(at, turn[1 - side]))
                passed[cut] = push(ref, ref, fwd_send.at[h, cut], fwd_recv.at[h, cut], peer(h, turn[side]))

        def wait_side(side):
            for k in range(count // 2, count):
                copies[side, order[side][k]].wait_recv()

        def wait_passed():
            for cut in range(count):
                passed[cut].wait_recv()

        return relay_on, wait_side, wait_passed

    back = []
    for h in range(2):
        for copy in up[h]:
            copy.wait_recv()

        def strip(cut, at, h=h):
            return out_ref.at[cut, core, outer[h], at, :, lanes_of[h]]

        back.append(spread(h, inner[h], inner_peer, strip, (pl.ds(0, 2), pl.ds(2, 2)), in_s, in_r, pass_s, pass_r))
    for side in range(2):
        hops[side].wait_recv()
        ref = relay.at[side]
        hops.append(
            push(ref, landing(ring(z, turn[1 - side]), side), hop_s.at[side, 1], hop_r.at[side, 1], stack[turn[side] - 1])
        )
        for half in range(2):
            hops.append(
                push(
                    columns(ring(z, turn[side]), half), landing(z, half),
                    hop_s.at[side, 2 + half], hop_r.at[side, 2 + half], stack[turn[side] - 1],
                )
            )
    for h in range(2):
        back[h][0](0)

    def give(h, group, at):
        ref = out_ref.at[:, core, group, :, :, lanes_of[h]]
        return push(ref, ref, give_s.at[h, at], give_r.at[h, at], twin)

    ahead, got = [], []
    for h in range(2):
        for side in range(2):
            back[h][1](side)
        back[h][2]()

        def block(cut, at, h=h):
            return out_ref.at[cut, core, at, :, :, lanes_of[h]]

        ahead.append(spread(h, outer[h], outer_peer, block, tuple(range(SIDE)), out_s, out_r, fwd_s, fwd_r))
    for h in range(2):
        got.append(give(h, outer[h], 0))
    for k in range(2):
        for h in range(2):
            ahead[h][0](k)
    for h in range(2):
        for side in range(2):
            ahead[h][1](side)
            got.append(give(h, ring(outer[h], turn[1 - side]), 1 + side))
    for h in range(2):
        ahead[h][2]()
        got.append(give(h, ring(outer[h], 2), 3))
    for copy in got + hops[2:]:
        copy.wait_recv()
    for copy in sent:
        copy.wait_send()


def gather_projected(part, turned):
    rows = part.shape[0]
    cols = turned.shape[0]
    share = cols // SIDE
    sem = pltpu.SemaphoreType.DMA
    pair = lambda *shape: [sem(shape), sem(shape)]
    vmem = pl.BlockSpec(memory_space=pltpu.VMEM)
    out, columns = pl.pallas_call(
        gather_kernel,
        out_shape=[
            jax.ShapeDtypeStruct((SIDE, 2, SIDE, SIDE, 16, RANK), jnp.float32),
            jax.ShapeDtypeStruct((share, SIDE * rows), jnp.float32),
        ],
        in_specs=[vmem, vmem],
        out_specs=[vmem, vmem],
        scratch_shapes=[
            pltpu.VMEM((SIDE, 64, RANK), jnp.float32),
            pltpu.VMEM((SIDE, 64, RANK), jnp.float32),
            pltpu.VMEM((2, 2, 32, HALF), jnp.float32),
            pltpu.VMEM((2, 2, 64, HALF), jnp.float32),
            pltpu.VMEM((2, SIDE, 16, HALF), jnp.float32),
            pltpu.VMEM((2, 3, 16, HALF), jnp.float32),
            pltpu.VMEM((2, share // 2, rows), jnp.float32),
            *pair(), *pair(2, 2), *pair(2, 2, 2), *pair(2, 3), *pair(2, 3), *pair(2, 2, 2), *pair(2, 2, SIDE),
            *pair(2, SIDE), *pair(2, SIDE), *pair(2, 2), *pair(2, SIDE),
        ],
        compiler_params=pltpu.CompilerParams(collective_id=0, has_side_effects=True, vmem_limit_bytes=28 * 2**20),
        cost_estimate=pl.CostEstimate(flops=10**6, bytes_accessed=12 * 2**20, transcendentals=0),
        name="gather_projected",
    )(part.reshape(2, SIDE, 64, RANK), turned)
    return out.reshape(SIDE * rows, RANK), columns


def norm_kernel(part_ref, out_ref, held, slots, pair_s, pair_r, one_s, one_r, two_s, two_r):
    z, x, y, core = place()
    twin = device(z, x, y, 1 - core)
    along_x = [device(z, ring(x, step), y, core) for step in range(1, SIDE)]
    along_y = [device(z, x, ring(y, step), core) for step in range(1, SIDE)]
    greet([twin] + along_x + along_y)
    swap = remote(part_ref, slots.at[0], pair_s, pair_r, twin)
    swap.start()
    swap.wait()
    held[0] = part_ref[...] + slots[0]
    for turn, (peers, send, recv) in enumerate(((along_x, one_s, one_r), (along_y, two_s, two_r))):
        copies = []
        for step in range(3):
            copy = remote(held.at[turn], slots.at[1 + 3 * turn + step], send.at[step], recv.at[step], peers[step])
            copy.start()
            copies.append(copy)
        for copy in copies:
            copy.wait()
        summed = held[turn] + slots[1 + 3 * turn] + slots[2 + 3 * turn] + slots[3 + 3 * turn]
        if turn == 0:
            held[1] = summed
        else:
            out_ref[...] = summed


def sum_norms(part):
    sem = pltpu.SemaphoreType.DMA
    tile = (8, BLK)
    out = pl.pallas_call(
        norm_kernel,
        out_shape=jax.ShapeDtypeStruct(tile, jnp.float32),
        in_specs=[pl.BlockSpec(memory_space=pltpu.VMEM)],
        out_specs=pl.BlockSpec(memory_space=pltpu.VMEM),
        scratch_shapes=[
            pltpu.VMEM((2,) + tile, jnp.float32),
            pltpu.VMEM((7,) + tile, jnp.float32),
            sem(()), sem(()), sem((3,)), sem((3,)), sem((3,)), sem((3,)),
        ],
        compiler_params=pltpu.CompilerParams(collective_id=1, has_side_effects=True),
        name="sum_norms",
    )(part.reshape(tile))
    return out.reshape(RANK)


NN = ((1,), (0,))
NT = ((1,), (1,))


def split(x):
    hi = x.astype(jnp.bfloat16)
    return hi, (x - hi.astype(jnp.float32)).astype(jnp.bfloat16)


def dot3(a, b, contract):
    one = functools.partial(
        lax.dot_general, dimension_numbers=(contract, ((), ())), preferred_element_type=jnp.float32
    )
    return one(a[0], b[0]) + (one(a[0], b[1]) + one(a[1], b[0]))


def mix_kernel(columns, proj, out_ref):
    deep = 512
    for at in range(0, proj.shape[0], deep):
        left = split(columns[:, at:at + deep])
        for c in range(0, RANK, 256):
            term = dot3(left, split(proj[at:at + deep, c:c + 256]), NN)
            if at == 0:
                out_ref[:, c:c + 256] = term
            else:
                out_ref[:, c:c + 256] += term


def mix(columns, projected):
    share, rows = columns.shape
    vmem = pl.BlockSpec(memory_space=pltpu.VMEM)
    return pl.pallas_call(
        mix_kernel,
        out_shape=jax.ShapeDtypeStruct((share, RANK), jnp.float32),
        in_specs=[vmem, vmem],
        out_specs=vmem,
        compiler_params=pltpu.CompilerParams(vmem_limit_bytes=24 * 2**20),
        cost_estimate=pl.CostEstimate(flops=6 * rows * share * RANK, bytes_accessed=12 * 2**20, transcendentals=0),
        name="mix",
    )(columns, projected)


def apply_kernel(mixed, inverse, right_ref, square_ref, hi, lo):
    @pl.when(pl.program_id(0) == 0)
    def _():
        hi[...], lo[...] = split(inverse[...])
        square_ref[...] = jnp.zeros_like(square_ref)

    left = split(mixed[...])
    for c in range(0, RANK, 256):
        deep = c + 256
        weight = (hi[c:deep, :deep], lo[c:deep, :deep])
        got = dot3((left[0][:, :deep], left[1][:, :deep]), weight, NT)
        right_ref[:, c:deep] = got
        square_ref[:, c:deep] += jnp.sum((got * got).reshape(-1, 8, 256), axis=0)


def apply_inverse(mixed, inverse):
    cols = mixed.shape[0]
    tall = cols // 4
    return pl.pallas_call(
        apply_kernel,
        grid=(4,),
        out_shape=[jax.ShapeDtypeStruct((cols, RANK), jnp.float32), jax.ShapeDtypeStruct((8, RANK), jnp.float32)],
        in_specs=[pl.BlockSpec((tall, RANK), lambda i: (i, 0)), pl.BlockSpec((RANK, RANK), lambda i: (0, 0))],
        out_specs=[pl.BlockSpec((tall, RANK), lambda i: (i, 0)), pl.BlockSpec((8, RANK), lambda i: (0, 0))],
        scratch_shapes=[pltpu.VMEM((RANK, RANK), jnp.bfloat16), pltpu.VMEM((RANK, RANK), jnp.bfloat16)],
        compiler_params=pltpu.CompilerParams(vmem_limit_bytes=32 * 2**20),
        cost_estimate=pl.CostEstimate(flops=8 * 10**9, bytes_accessed=18 * 2**20, transcendentals=0),
        name="apply_inverse",
    )(mixed, inverse)


def dot(a, b, contract, precision):
    return lax.dot_general(a, b, (contract, ((), ())), precision=precision, preferred_element_type=jnp.float32)


def body(momentum, gradient, basis):
    rows = momentum.shape[0]
    total_cols = basis.shape[0] * lax.axis_size("col")
    buffer = momentum + gradient.astype(jnp.float32)
    local_proj = dot(buffer, basis, NN, high)
    projected, columns = gather_projected(local_proj, buffer.T)
    mixed = lax.all_gather(mix(columns, projected), "row", axis=0, tiled=True)
    own_rows = lax.dynamic_slice_in_dim(projected, lax.axis_index("row") * rows, rows, 0)
    inverse = inverse_factor(projected)
    orthonormal = dot(own_rows, inverse, NT, high)
    right_factor, squares = apply_inverse(mixed, inverse)
    squares = sum_norms(jnp.sum(squares, axis=0))
    col_scale = jnp.sqrt(squares / total_cols + 1e-06)
    new_basis = right_factor / col_scale[None, :]
    feedback = dot(orthonormal, right_factor, NT, lax.Precision.DEFAULT)
    new_momentum = buffer - 0.05 * feedback
    update = dot(orthonormal, new_basis, NT, high)
    return (new_momentum, new_basis, update.astype(jnp.bfloat16))


def solution(mesh):
    in_specs = (P("row", "col"), P("row", "col"), P("col", None))
    out_specs = (P("row", "col"), P("col", None), P("row", "col"))
    return jax.shard_map(body, mesh=mesh, in_specs=in_specs, out_specs=out_specs, check_vma=False)
```

```python
import functools
import jax
import jax.numpy as jnp
from jax import lax
from jax.experimental import pallas as pl
from jax.experimental.pallas import tpu as pltpu
from jax.sharding import PartitionSpec as P

highest = lax.Precision.HIGHEST
high = lax.Precision.HIGH
MESH = pl.DeviceIdType.MESH
RANK = 1024
BLK = 128
BASE = 32
SIDE = 4
HALF = RANK // 2


def dot_tn(a, b):
    return lax.dot_general(a, b, (((0,), (0,)), ((), ())), precision=highest, preferred_element_type=jnp.float32)

def dot_nn(a, b):
    return lax.dot_general(a, b, (((1,), (0,)), ((), ())), precision=highest, preferred_element_type=jnp.float32)

def lanes(col):
    return jnp.broadcast_to(col, (8, BLK))

def eliminate(tiles, off, fill):
    lane = lax.broadcasted_iota(jnp.int32, (8, BLK), 1)
    sub = lax.broadcasted_iota(jnp.int32, (8, BLK), 0)
    n = len(tiles)
    done = []
    for g in range(n):
        first = off + 8 * g
        cols = [[lanes(tiles[t][:, first + j:first + j + 1]) for j in range(8)] for t in range(g, n)]
        inside = (lane >= first) & (lane < first + 8)
        tiles[g] = jnp.where(inside, jnp.where(lane - first == sub, 1.0, 0.0), tiles[g])
        for t in range(g + 1, n):
            tiles[t] = jnp.where(inside, 0.0, tiles[t])
        el = [[jnp.broadcast_to(cols[0][j][i:i + 1, :], (8, BLK)) if j >= i else None for j in range(8)] for i in range(8)]
        scale = jnp.zeros((8, BLK), jnp.float32)
        for i in range(8):
            rinv = pl.reciprocal(el[i][i], approx=True)
            rinv = rinv * (2.0 - el[i][i] * rinv)
            scale = jnp.where(sub == i, el[i][i], scale)
            mult = [None] * 8
            for j in range(i + 1, 8):
                mult[j] = el[i][j] * rinv
                for l in range(j, 8):
                    el[j][l] = el[j][l] - mult[j] * el[i][l]
            row = jnp.broadcast_to(tiles[g][i:i + 1, :], (8, BLK)) * rinv
            for t in range(g, n):
                c = cols[t - g][i]
                for j in range(i + 1, 8):
                    cols[t - g][j] = cols[t - g][j] - c * mult[j]
                if t == g:
                    c = jnp.where(sub > i, c, 0.0)
                tiles[t] = tiles[t] - c * row
        done.append(tiles[g] * lax.rsqrt(scale))
        fill()
    full = jnp.concatenate(done, axis=0)
    ln = lax.broadcasted_iota(jnp.int32, full.shape, 1) - off
    rw = lax.broadcasted_iota(jnp.int32, full.shape, 0)
    return jnp.where((ln > rw) & (ln < 8 * n), 0.0, full)

def invert_block(work, at, fill):
    lane = lax.broadcasted_iota(jnp.int32, (BLK, BLK), 1)
    blk = work[pl.ds(at, BLK), pl.ds(at, BLK)]
    parts = []
    for b in range(BLK // BASE):
        lo = b * BASE
        rows = blk[0:BASE, :]
        tiles = [rows[8 * t:8 * t + 8, :] for t in range(BASE // 8)]
        s = eliminate(tiles, lo, fill)
        parts.append(s)
        if lo + BASE < BLK:
            upd = dot_tn(s, s)
            rest = blk[BASE:, :]
            ln = lax.broadcasted_iota(jnp.int32, rest.shape, 1)
            blk = jnp.where((ln >= lo) & (ln < lo + BASE), 0.0, rest) - upd[lo + BASE:, :]
    f = jnp.concatenate(parts, axis=0)
    row = lax.broadcasted_iota(jnp.int32, (BLK, BLK), 0)
    return jnp.where(row >= lane, f, 0.0)


NN = ((1,), (0,))
NT = ((1,), (1,))


def split(x):
    hi = x.astype(jnp.bfloat16)
    return hi, (x - hi.astype(jnp.float32)).astype(jnp.bfloat16)


def dot3(a, b, contract):
    one = functools.partial(
        lax.dot_general, dimension_numbers=(contract, ((), ())), preferred_element_type=jnp.float32
    )
    return one(a[0], b[0]) + (one(a[0], b[1]) + one(a[1], b[0]))

TN = ((0,), (0,))


def inverse_kernel(place_ref, proj_ref, full_ref, out_ref, own_ref, ortho_ref, work, hi, lo_part, full_hi, full_lo):
    nb = RANK // BLK
    wide = 2 * BLK
    queue = []

    def fill():
        if queue:
            queue.pop(0)()

    def gram(pair, col):
        rows, cols = slice(pair * wide, pair * wide + wide), slice(col * wide, col * wide + wide)
        work[rows, cols] = dot3((hi[:, rows], lo_part[:, rows]), (hi[:, cols], lo_part[:, cols]), TN)

    def own(col):
        cols = slice(col * wide, col * wide + wide)
        own_ref[:, cols] = dot3((full_hi[...], full_lo[...]), (hi[:, cols], lo_part[:, cols]), NN)

    def right(i, first, last, lo, up):
        at = i * BLK
        left = slice(first * BLK, last * BLK)
        work[at:at + BLK, lo:up] -= dot_tn(work[left, at:at + BLK], work[left, lo:up])

    def left(i, c, last):
        at, lo = i * BLK, c * BLK
        rows = slice(lo, last * BLK)
        work[at:at + BLK, lo:lo + BLK] = -dot3(split(work[rows, at:at + BLK]), split(work[rows, lo:lo + BLK]), TN)

    def ortho(pair):
        cols = slice(pair * wide, pair * wide + wide)
        mine = pl.ds(pl.multiple_of(place_ref[0] * ortho_ref.shape[0], 512), ortho_ref.shape[0])
        deep = pair * wide + wide
        ortho_ref[:, cols] = dot3((hi[mine, :deep], lo_part[mine, :deep]), split(out_ref[cols, :deep]), NT)

    def later(f, *args):
        queue.append(functools.partial(f, *args))

    hi[...], lo_part[...] = split(proj_ref[...])
    full_hi[...], full_lo[...] = split(full_ref[...])
    for col in range(RANK // wide):
        gram(0, col)
    extra = [functools.partial(own, col) for col in range(RANK // wide)]
    for j in range(nb):
        at = j * BLK
        if j % 2 == 0 and j + 2 < nb:
            for col in range(j // 2 + 1, RANK // wide):
                later(gram, j // 2 + 1, col)
        if j and j + 1 < nb:
            for lo in range(at + BLK, RANK, wide):
                later(right, j + 1, 0, j, lo, min(lo + wide, RANK))
            for c in range(j):
                later(left, j + 1, c, j)
        if j == nb - 1 or (j % 2 and extra):
            queue.extend(extra if j == nb - 1 else extra[:1])
            extra = extra[1:]
        if j and j % 2 == 0:
            later(ortho, j // 2 - 1)
        f = invert_block(work, at, fill)
        while queue:
            fill()
        if at:
            work[at:at + BLK, 0:at] = dot3(split(f), split(work[at:at + BLK, 0:at]), NN)
        if j + 1 < nb:
            work[at:at + BLK, at + BLK:] = dot_nn(f, work[at:at + BLK, at + BLK:])
        work[at:at + BLK, at:at + BLK] = f
        out_ref[at:at + BLK, 0:at + BLK] = work[at:at + BLK, 0:at + BLK]
        if j + 1 < nb:
            out_ref[at:at + BLK, at + BLK:] = jnp.zeros((BLK, RANK - at - BLK), jnp.float32)
            right(j + 1, j, j + 1, at + BLK, RANK)
            nxt = at + BLK
            if at:
                work[nxt:nxt + BLK, 0:at] -= dot3(
                    split(work[at:at + BLK, nxt:nxt + BLK]), split(work[at:at + BLK, 0:at]), TN
                )
            work[nxt:nxt + BLK, at:nxt] = -dot3(split(work[at:at + BLK, nxt:nxt + BLK]), split(f), TN)
    ortho(RANK // wide - 1)


def inverse_factor(place, projected, full):
    rows = projected.shape[0]
    tall = full.shape[0]
    vmem = pl.BlockSpec(memory_space=pltpu.VMEM)
    return pl.pallas_call(
        inverse_kernel,
        out_shape=[
            jax.ShapeDtypeStruct((RANK, RANK), jnp.float32),
            jax.ShapeDtypeStruct((tall, RANK), jnp.float32),
            jax.ShapeDtypeStruct((rows // SIDE, RANK), jnp.float32),
        ],
        in_specs=[pl.BlockSpec(memory_space=pltpu.SMEM), vmem, vmem],
        out_specs=[vmem, vmem, vmem],
        scratch_shapes=[
            pltpu.VMEM((RANK, RANK), jnp.float32),
            pltpu.VMEM((rows, RANK), jnp.bfloat16), pltpu.VMEM((rows, RANK), jnp.bfloat16),
            pltpu.VMEM((tall, rows), jnp.bfloat16), pltpu.VMEM((tall, rows), jnp.bfloat16),
        ],
        compiler_params=pltpu.CompilerParams(vmem_limit_bytes=32 * 2**20),
        cost_estimate=pl.CostEstimate(flops=60 * 10**9, bytes_accessed=12 * 2**20, transcendentals=0),
        name="inverse_factor",
    )(place, projected, full)


def place():
    col = lax.axis_index("col")
    return lax.axis_index("row"), col // (2 * SIDE), lax.rem(col // 2, SIDE), lax.rem(col, 2)


def ring(at, step):
    return lax.rem(at + step, SIDE)


def device(z, x, y, core):
    return (z, (x * SIDE + y) * 2 + core)


def greet(peers):
    barrier = pltpu.get_barrier_semaphore()
    for peer in peers:
        pl.semaphore_signal(barrier, inc=1, device_id=peer, device_id_type=MESH)
    pl.semaphore_wait(barrier, len(peers))


def remote(src, dst, send, recv, to):
    return pltpu.make_async_remote_copy(
        src_ref=src, dst_ref=dst, send_sem=send, recv_sem=recv, device_id=to, device_id_type=MESH
    )


def gather_kernel(part_ref, turned_ref, out_ref, rows_ref, full_ref, paired, total, far, near, sums, slots2, relay, *sems):
    (pair_s, pair_r, far_s, far_r, near_s, near_r, rs2_s, rs2_r, z_s, z_r, in_s, in_r, out_s, out_r,
     fwd_s, fwd_r, hop_s, hop_r, pass_s, pass_r, give_s, give_r, all_s, all_r, on_s, on_r) = sems
    z, x, y, core = place()
    lanes_of = (pl.ds(0, HALF), pl.ds(HALF, HALF))
    outer = (x, y)
    inner = (y, x)

    def outer_peer(h, step):
        return device(z, ring(x, step), y, core) if h == 0 else device(z, x, ring(y, step), core)

    def inner_peer(h, step):
        return outer_peer(1 - h, step)

    turn = (1, SIDE - 1)
    twin = device(z, x, y, 1 - core)
    sides = [outer_peer(h, step) for h in range(2) for step in range(1, SIDE)]
    stack = [device(ring(z, step), x, y, core) for step in range(1, SIDE)]
    greet([twin] + sides + stack)
    sent = []

    def push(*args):
        copy = remote(*args)
        copy.start()
        sent.append(copy)
        return copy

    swap = push(part_ref.at[1 - core], paired, pair_s, pair_r, twin)

    share, slab_rows = rows_ref.shape[0], turned_ref.shape[1]
    split_at = share // 16 * 8
    parts = ((0, split_at), (split_at, share - split_at))

    def columns(to, side):
        return turned_ref.at[pl.ds(pl.multiple_of(to * share + parts[side][0], 8), parts[side][1]), :]

    def slab_lanes(slab):
        return pl.ds(pl.multiple_of(slab * slab_rows, 128), slab_rows)

    held = (relay.at[0, pl.ds(0, parts[0][1])], relay.at[1, pl.ds(0, parts[1][1])])
    hops = []
    for side in range(2):
        hops.append(
            push(columns(ring(z, 2), side), held[side], hop_s.at[side, 0], hop_r.at[side, 0], stack[turn[side] - 1])
        )

    def landing(slab, side):
        return rows_ref.at[pl.ds(*parts[side]), slab_lanes(slab)]

    wide = full_ref.shape[0]
    cut_rows = wide // SIDE
    full_ref[:, slab_lanes(z)] = turned_ref[turned_ref.shape[0] - wide:, :]
    around, onward = {}, {}

    def stack_block(cut, slab):
        return full_ref.at[pl.ds(cut * cut_rows, cut_rows), slab_lanes(slab)]

    def send_around(k):
        for side in range(2):
            cut = (2 * side + k) % SIDE
            ref = stack_block(cut, z)
            around[side, cut] = push(ref, ref, all_s.at[side, cut], all_r.at[side, cut], stack[turn[side] - 1])

    def send_onward(k):
        for side in range(2):
            cut = 2 * side + k
            around[side, cut].wait_recv()
            ref = stack_block(cut, ring(z, turn[1 - side]))
            onward[cut] = push(ref, ref, on_s.at[cut], on_r.at[cut], stack[turn[side] - 1])

    send_around(0)
    swap.wait_recv()
    total[...] = part_ref[core] + paired[...]
    half_rows = (pl.ds(0, 32), pl.ds(32, 32))
    first, early = {}, {}
    for h in range(2):
        for side in range(2):
            first[h, side] = push(
                total.at[ring(outer[h], 2), half_rows[side], lanes_of[h]], far.at[h, side],
                far_s.at[h, side], far_r.at[h, side], outer_peer(h, turn[side]),
            )
        for side in range(2):
            early[h, side] = push(
                total.at[ring(outer[h], turn[side]), half_rows[1 - side], lanes_of[h]], near.at[h, side, half_rows[1 - side]],
                near_s.at[h, side, 0], near_r.at[h, side, 0], outer_peer(h, turn[side]),
            )
    late = {}
    for h in range(2):
        for side in range(2):
            first[h, side].wait_recv()
            block = ring(outer[h], turn[side])
            total[block, 32 * side:32 * side + 32, h * HALF:(h + 1) * HALF] += far[h, side]
            late[h, side] = push(
                total.at[block, half_rows[side], lanes_of[h]], near.at[h, side, half_rows[side]],
                near_s.at[h, side, 1], near_r.at[h, side, 1], outer_peer(h, turn[side]),
            )
    second = [[None] * 3, [None] * 3]
    for h in range(2):
        for side in range(2):
            early[h, side].wait_recv()
            late[h, side].wait_recv()
        summed = total[outer[h], :, h * HALF:(h + 1) * HALF] + near[h, 0] + near[h, 1]
        sums[h] = summed.reshape(SIDE, 16, HALF)
        for step in (2, 1, 3):
            second[h][step - 1] = push(
                sums.at[h, ring(inner[h], step)], slots2.at[h, step - 1],
                rs2_s.at[h, step - 1], rs2_r.at[h, step - 1], inner_peer(h, step),
            )

    up = [[None] * 3, [None] * 3]
    for h in range(2):
        for copy in second[h]:
            copy.wait_recv()
        done = sums[h, inner[h]] + slots2[h, 0] + slots2[h, 1] + slots2[h, 2]
        out_ref[z, core, outer[h], inner[h], :, h * HALF:(h + 1) * HALF] = done
        own = out_ref.at[z, core, outer[h], inner[h], :, lanes_of[h]]
        for step in (2, 1, 3):
            up[h][step - 1] = push(own, own, z_s.at[h, step - 1], z_r.at[h, step - 1], stack[step - 1])

    rows_ref[:, pl.ds(pl.multiple_of(z * slab_rows, 128), slab_rows)] = turned_ref[
        pl.ds(pl.multiple_of(z * share, 8), share), :
    ]

    def spread(h, at, peer, ref_of, cuts, send, recv, fwd_send, fwd_recv):
        count = len(cuts)
        order = (list(range(count)), list(range(count // 2, count)) + list(range(count // 2)))
        copies, passed = {}, {}
        for k in range(count):
            for side in range(2):
                cut = order[side][k]
                ref = ref_of(cuts[cut], at)
                copies[side, cut] = push(ref, ref, send.at[h, side, cut], recv.at[h, side, cut], peer(h, turn[side]))

        def relay_on(k):
            for side in range(2):
                cut = order[side][k]
                copies[side, cut].wait_recv()
                ref = ref_of(cuts[cut], ring(at, turn[1 - side]))
                passed[cut] = push(ref, ref, fwd_send.at[h, cut], fwd_recv.at[h, cut], peer(h, turn[side]))

        def wait_side(side):
            for k in range(count // 2, count):
                copies[side, order[side][k]].wait_recv()

        def wait_passed():
            for cut in range(count):
                passed[cut].wait_recv()

        return relay_on, wait_side, wait_passed

    back = []
    for h in range(2):
        for copy in up[h]:
            copy.wait_recv()

        def strip(cut, at, h=h):
            return out_ref.at[cut, core, outer[h], at, :, lanes_of[h]]

        back.append(spread(h, inner[h], inner_peer, strip, (pl.ds(0, 2), pl.ds(2, 2)), in_s, in_r, pass_s, pass_r))
    for side in range(2):
        hops[side].wait_recv()
        hops.append(
            push(held[side], landing(ring(z, turn[1 - side]), side), hop_s.at[side, 1], hop_r.at[side, 1], stack[turn[side] - 1])
        )
        for half in range(2):
            hops.append(
                push(
                    columns(ring(z, turn[side]), half), landing(z, half),
                    hop_s.at[side, 2 + half], hop_r.at[side, 2 + half], stack[turn[side] - 1],
                )
            )
    send_around(1)
    send_around(2)
    for h in range(2):
        back[h][0](0)
    send_around(3)

    def give(h, group, at):
        ref = out_ref.at[:, core, group, :, :, lanes_of[h]]
        return push(ref, ref, give_s.at[h, at], give_r.at[h, at], twin)

    ahead, got = [], []
    for h in range(2):
        for side in range(2):
            back[h][1](side)
        back[h][2]()

        def block(cut, at, h=h):
            return out_ref.at[cut, core, at, :, :, lanes_of[h]]

        ahead.append(spread(h, outer[h], outer_peer, block, tuple(range(SIDE)), out_s, out_r, fwd_s, fwd_r))
    for h in range(2):
        got.append(give(h, outer[h], 0))
    send_onward(0)
    send_onward(1)
    for k in range(2):
        for h in range(2):
            ahead[h][0](k)
    for h in range(2):
        for side in range(2):
            ahead[h][1](side)
            got.append(give(h, ring(outer[h], turn[1 - side]), 1 + side))
    for h in range(2):
        ahead[h][2]()
        got.append(give(h, ring(outer[h], 2), 3))
    for side in range(2):
        for k in (2, 3):
            around[side, (2 * side + k) % SIDE].wait_recv()
    for copy in got + hops[2:] + list(onward.values()):
        copy.wait_recv()
    for copy in sent:
        copy.wait_send()


def gather_projected(part, turned, wide):
    rows = part.shape[0]
    cols = turned.shape[0]
    share = (cols - wide) // SIDE
    sem = pltpu.SemaphoreType.DMA
    pair = lambda *shape: [sem(shape), sem(shape)]
    vmem = pl.BlockSpec(memory_space=pltpu.VMEM)
    out, columns, full = pl.pallas_call(
        gather_kernel,
        out_shape=[
            jax.ShapeDtypeStruct((SIDE, 2, SIDE, SIDE, 16, RANK), jnp.float32),
            jax.ShapeDtypeStruct((share, SIDE * rows), jnp.float32),
            jax.ShapeDtypeStruct((wide, SIDE * rows), jnp.float32),
        ],
        in_specs=[vmem, vmem],
        out_specs=[vmem, vmem, vmem],
        scratch_shapes=[
            pltpu.VMEM((SIDE, 64, RANK), jnp.float32),
            pltpu.VMEM((SIDE, 64, RANK), jnp.float32),
            pltpu.VMEM((2, 2, 32, HALF), jnp.float32),
            pltpu.VMEM((2, 2, 64, HALF), jnp.float32),
            pltpu.VMEM((2, SIDE, 16, HALF), jnp.float32),
            pltpu.VMEM((2, 3, 16, HALF), jnp.float32),
            pltpu.VMEM((2, share - share // 16 * 8, rows), jnp.float32),
            *pair(), *pair(2, 2), *pair(2, 2, 2), *pair(2, 3), *pair(2, 3), *pair(2, 2, 2), *pair(2, 2, SIDE),
            *pair(2, SIDE), *pair(2, SIDE), *pair(2, 2), *pair(2, SIDE), *pair(2, SIDE), *pair(SIDE),
        ],
        compiler_params=pltpu.CompilerParams(collective_id=0, has_side_effects=True, vmem_limit_bytes=28 * 2**20),
        cost_estimate=pl.CostEstimate(flops=10**6, bytes_accessed=12 * 2**20, transcendentals=0),
        name="gather_projected",
    )(part.reshape(2, SIDE, 64, RANK), turned)
    return out.reshape(SIDE * rows, RANK), columns, full


def norm_kernel(part_ref, out_ref, held, slots, pair_s, pair_r, one_s, one_r, two_s, two_r):
    z, x, y, core = place()
    twin = device(z, x, y, 1 - core)
    along_x = [device(z, ring(x, step), y, core) for step in range(1, SIDE)]
    along_y = [device(z, x, ring(y, step), core) for step in range(1, SIDE)]
    greet([twin] + along_x + along_y)
    swap = remote(part_ref, slots.at[0], pair_s, pair_r, twin)
    swap.start()
    swap.wait()
    held[0] = part_ref[...] + slots[0]
    for turn, (peers, send, recv) in enumerate(((along_x, one_s, one_r), (along_y, two_s, two_r))):
        copies = []
        for step in range(3):
            copy = remote(held.at[turn], slots.at[1 + 3 * turn + step], send.at[step], recv.at[step], peers[step])
            copy.start()
            copies.append(copy)
        for copy in copies:
            copy.wait()
        summed = held[turn] + slots[1 + 3 * turn] + slots[2 + 3 * turn] + slots[3 + 3 * turn]
        if turn == 0:
            held[1] = summed
        else:
            out_ref[...] = summed


def sum_norms(part):
    sem = pltpu.SemaphoreType.DMA
    tile = (8, BLK)
    out = pl.pallas_call(
        norm_kernel,
        out_shape=jax.ShapeDtypeStruct(tile, jnp.float32),
        in_specs=[pl.BlockSpec(memory_space=pltpu.VMEM)],
        out_specs=pl.BlockSpec(memory_space=pltpu.VMEM),
        scratch_shapes=[
            pltpu.VMEM((2,) + tile, jnp.float32),
            pltpu.VMEM((7,) + tile, jnp.float32),
            sem(()), sem(()), sem((3,)), sem((3,)), sem((3,)), sem((3,)),
        ],
        compiler_params=pltpu.CompilerParams(collective_id=1, has_side_effects=True),
        name="sum_norms",
    )(part.reshape(tile))
    return out.reshape(RANK)


def apply_kernel(share, spread, own, inverse, right_ref, square_ref, hi, lo):
    at = pl.program_id(0)

    @pl.when(at == 0)
    def _():
        hi[...], lo[...] = split(inverse[...])
        square_ref[...] = jnp.zeros_like(square_ref)

    def times(mixed):
        left = split(mixed)
        for c in range(0, RANK, 256):
            deep = c + 256
            weight = (hi[c:deep, :deep], lo[c:deep, :deep])
            got = dot3((left[0][:, :deep], left[1][:, :deep]), weight, NT)
            right_ref[:, c:deep] = got
            square_ref[:, c:deep] += jnp.sum((got * got).reshape(-1, 8, 256), axis=0)

    @pl.when(at < share)
    def _():
        times(spread[...])

    @pl.when(at == share)
    def _():
        times(own[...])


def apply_inverse(spread, own, inverse):
    tall = own.shape[0]
    share = spread.shape[0] // tall
    cols = spread.shape[0] + tall
    return pl.pallas_call(
        functools.partial(apply_kernel, share),
        grid=(share + 1,),
        out_shape=[jax.ShapeDtypeStruct((cols, RANK), jnp.float32), jax.ShapeDtypeStruct((8, RANK), jnp.float32)],
        in_specs=[
            pl.BlockSpec((tall, RANK), lambda i: (jnp.minimum(i, share - 1), 0)),
            pl.BlockSpec((tall, RANK), lambda i: (0, 0)),
            pl.BlockSpec(memory_space=pltpu.VMEM),
        ],
        out_specs=[pl.BlockSpec((tall, RANK), lambda i: (i, 0)), pl.BlockSpec((8, RANK), lambda i: (0, 0))],
        scratch_shapes=[pltpu.VMEM((RANK, RANK), jnp.bfloat16), pltpu.VMEM((RANK, RANK), jnp.bfloat16)],
        compiler_params=pltpu.CompilerParams(vmem_limit_bytes=24 * 2**20),
        cost_estimate=pl.CostEstimate(flops=8 * 10**9, bytes_accessed=18 * 2**20, transcendentals=0),
        name="apply_inverse",
    )(spread, own, inverse)


def dot(a, b, contract, precision):
    return lax.dot_general(a, b, (contract, ((), ())), precision=precision, preferred_element_type=jnp.float32)


def body(momentum, gradient, basis):
    total_cols = basis.shape[0] * lax.axis_size("col")
    buffer = lax.optimization_barrier(momentum + gradient.astype(jnp.float32))
    local_proj = dot(buffer, basis, NN, high)
    projected, columns, full = gather_projected(local_proj, buffer.T, buffer.shape[1] // 4)
    spread = lax.all_gather(dot(columns, projected, NN, high), "row", axis=0, tiled=True)
    place_z = lax.axis_index("row").astype(jnp.int32).reshape(1)
    inverse, own, orthonormal = inverse_factor(place_z, projected, full)
    right_factor, squares = apply_inverse(spread, own, inverse)
    squares = sum_norms(jnp.sum(squares, axis=0))
    col_scale = jnp.sqrt(squares / total_cols + 1e-06)
    new_basis = right_factor / col_scale[None, :]
    feedback = dot(orthonormal, right_factor, NT, lax.Precision.DEFAULT)
    new_momentum = buffer - 0.05 * feedback
    update = dot(orthonormal, new_basis, NT, high)
    return (new_momentum, new_basis, update.astype(jnp.bfloat16))


def solution(mesh):
    in_specs = (P("row", "col"), P("row", "col"), P("col", None))
    out_specs = (P("row", "col"), P("col", None), P("row", "col"))
    return jax.shard_map(body, mesh=mesh, in_specs=in_specs, out_specs=out_specs, check_vma=False)
```

```python
import functools
import jax
import jax.numpy as jnp
from jax import lax
from jax.experimental import pallas as pl
from jax.experimental.pallas import tpu as pltpu
from jax.sharding import PartitionSpec as P

highest = lax.Precision.HIGHEST
high = lax.Precision.HIGH
MESH = pl.DeviceIdType.MESH
RANK = 1024
BLK = 128
BASE = 32
SIDE = 4
HALF = RANK // 2
SHARE = 320
WINDOW = 384


def dot_tn(a, b):
    return lax.dot_general(a, b, (((0,), (0,)), ((), ())), precision=highest, preferred_element_type=jnp.float32)

def dot_nn(a, b):
    return lax.dot_general(a, b, (((1,), (0,)), ((), ())), precision=highest, preferred_element_type=jnp.float32)

def lanes(col):
    return jnp.broadcast_to(col, (8, BLK))

def eliminate(tiles, off, fill):
    lane = lax.broadcasted_iota(jnp.int32, (8, BLK), 1)
    sub = lax.broadcasted_iota(jnp.int32, (8, BLK), 0)
    n = len(tiles)
    done = []
    for g in range(n):
        first = off + 8 * g
        cols = [[lanes(tiles[t][:, first + j:first + j + 1]) for j in range(8)] for t in range(g, n)]
        inside = (lane >= first) & (lane < first + 8)
        tiles[g] = jnp.where(inside, jnp.where(lane - first == sub, 1.0, 0.0), tiles[g])
        for t in range(g + 1, n):
            tiles[t] = jnp.where(inside, 0.0, tiles[t])
        el = [[jnp.broadcast_to(cols[0][j][i:i + 1, :], (8, BLK)) if j >= i else None for j in range(8)] for i in range(8)]
        scale = jnp.zeros((8, BLK), jnp.float32)
        for i in range(8):
            rinv = pl.reciprocal(el[i][i], approx=True)
            rinv = rinv * (2.0 - el[i][i] * rinv)
            scale = jnp.where(sub == i, el[i][i], scale)
            mult = [None] * 8
            for j in range(i + 1, 8):
                mult[j] = el[i][j] * rinv
                for l in range(j, 8):
                    el[j][l] = el[j][l] - mult[j] * el[i][l]
            row = jnp.broadcast_to(tiles[g][i:i + 1, :], (8, BLK)) * rinv
            for t in range(g, n):
                c = cols[t - g][i]
                for j in range(i + 1, 8):
                    cols[t - g][j] = cols[t - g][j] - c * mult[j]
                if t == g:
                    c = jnp.where(sub > i, c, 0.0)
                tiles[t] = tiles[t] - c * row
        done.append(tiles[g] * lax.rsqrt(scale))
        fill()
    full = jnp.concatenate(done, axis=0)
    ln = lax.broadcasted_iota(jnp.int32, full.shape, 1) - off
    rw = lax.broadcasted_iota(jnp.int32, full.shape, 0)
    return jnp.where((ln > rw) & (ln < 8 * n), 0.0, full)

def invert_block(work, at, fill):
    lane = lax.broadcasted_iota(jnp.int32, (BLK, BLK), 1)
    blk = work[pl.ds(at, BLK), pl.ds(at, BLK)]
    parts = []
    for b in range(BLK // BASE):
        lo = b * BASE
        rows = blk[0:BASE, :]
        tiles = [rows[8 * t:8 * t + 8, :] for t in range(BASE // 8)]
        s = eliminate(tiles, lo, fill)
        parts.append(s)
        if lo + BASE < BLK:
            upd = dot_tn(s, s)
            rest = blk[BASE:, :]
            ln = lax.broadcasted_iota(jnp.int32, rest.shape, 1)
            blk = jnp.where((ln >= lo) & (ln < lo + BASE), 0.0, rest) - upd[lo + BASE:, :]
    f = jnp.concatenate(parts, axis=0)
    row = lax.broadcasted_iota(jnp.int32, (BLK, BLK), 0)
    return jnp.where(row >= lane, f, 0.0)


NN = ((1,), (0,))
NT = ((1,), (1,))


def split(x):
    hi = x.astype(jnp.bfloat16)
    return hi, (x - hi.astype(jnp.float32)).astype(jnp.bfloat16)


def dot3(a, b, contract):
    one = functools.partial(
        lax.dot_general, dimension_numbers=(contract, ((), ())), preferred_element_type=jnp.float32
    )
    return one(a[0], b[0]) + (one(a[0], b[1]) + one(a[1], b[0]))

TN = ((0,), (0,))


def inverse_kernel(place_ref, proj_hbm, full_hbm, out_hbm, own_hbm, ortho_hbm, proj_ref, full_ref, out_ref, own_ref, ortho_ref,
                   work, hi, lo_part, full_hi, full_lo, proj_sem, full_sem, out_sem, own_sem, ortho_sem):
    nb = RANK // BLK
    wide = 2 * BLK
    queue = []

    def fill():
        if queue:
            queue.pop(0)()

    def gram(pair, col):
        rows, cols = slice(pair * wide, pair * wide + wide), slice(col * wide, col * wide + wide)
        work[rows, cols] = dot3((hi[:, rows], lo_part[:, rows]), (hi[:, cols], lo_part[:, cols]), TN)

    def own(col):
        cols = slice(col * wide, col * wide + wide)
        own_ref[:, cols] = dot3((full_hi[...], full_lo[...]), (hi[:, cols], lo_part[:, cols]), TN)
        if col == RANK // wide - 1:
            store(own_ref, own_hbm, own_sem)

    def right(i, first, last, lo, up):
        at = i * BLK
        left = slice(first * BLK, last * BLK)
        work[at:at + BLK, lo:up] -= dot_tn(work[left, at:at + BLK], work[left, lo:up])

    def left(i, c, last):
        at, lo = i * BLK, c * BLK
        rows = slice(lo, last * BLK)
        work[at:at + BLK, lo:lo + BLK] = -dot3(split(work[rows, at:at + BLK]), split(work[rows, lo:lo + BLK]), TN)

    def ortho(pair):
        cols = slice(pair * wide, pair * wide + wide)
        mine = pl.ds(pl.multiple_of(place_ref[0] * ortho_ref.shape[0], 512), ortho_ref.shape[0])
        deep = pair * wide + wide
        ortho_ref[:, cols] = dot3((hi[mine, :deep], lo_part[mine, :deep]), split(out_ref[cols, :deep]), NT)

    def later(f, *args):
        queue.append(functools.partial(f, *args))

    stores = []

    def store(src, dst, sem):
        copy = pltpu.make_async_copy(src, dst, sem)
        copy.start()
        stores.append(copy)

    chunk = proj_ref.shape[0] // SIDE
    loads = [
        pltpu.make_async_copy(proj_hbm.at[pl.ds(i * chunk, chunk)], proj_ref.at[pl.ds(i * chunk, chunk)], proj_sem.at[i])
        for i in range(SIDE)
    ] + [pltpu.make_async_copy(full_hbm, full_ref, full_sem)]
    for copy in loads:
        copy.start()
    for i in range(SIDE):
        loads[i].wait()
        part = slice(i * chunk, i * chunk + chunk)
        hi[part, :], lo_part[part, :] = split(proj_ref[part, :])
    loads[SIDE].wait()
    full_hi[...], full_lo[...] = split(full_ref[...])
    for col in range(RANK // wide):
        gram(0, col)
    extra = [functools.partial(own, col) for col in range(RANK // wide)]
    for j in range(nb):
        at = j * BLK
        if j % 2 == 0 and j + 2 < nb:
            for col in range(j // 2 + 1, RANK // wide):
                later(gram, j // 2 + 1, col)
        if j and j + 1 < nb:
            for lo in range(at + BLK, RANK, wide):
                later(right, j + 1, 0, j, lo, min(lo + wide, RANK))
            for c in range(j):
                later(left, j + 1, c, j)
        if j == nb - 1 or (j % 2 and extra):
            queue.extend(extra if j == nb - 1 else extra[:1])
            extra = extra[1:]
        if j and j % 2 == 0:
            later(ortho, j // 2 - 1)
        f = invert_block(work, at, fill)
        while queue:
            fill()
        if at:
            work[at:at + BLK, 0:at] = dot3(split(f), split(work[at:at + BLK, 0:at]), NN)
        if j + 1 < nb:
            work[at:at + BLK, at + BLK:] = dot_nn(f, work[at:at + BLK, at + BLK:])
        work[at:at + BLK, at:at + BLK] = f
        out_ref[at:at + BLK, 0:at + BLK] = work[at:at + BLK, 0:at + BLK]
        if j + 1 == nb:
            store(out_ref.at[pl.ds(at, BLK)], out_hbm.at[pl.ds(at, BLK)], out_sem.at[j])
        if j + 1 < nb:
            out_ref[at:at + BLK, at + BLK:] = jnp.zeros((BLK, RANK - at - BLK), jnp.float32)
            store(out_ref.at[pl.ds(at, BLK)], out_hbm.at[pl.ds(at, BLK)], out_sem.at[j])
            right(j + 1, j, j + 1, at + BLK, RANK)
            nxt = at + BLK
            if at:
                work[nxt:nxt + BLK, 0:at] -= dot3(
                    split(work[at:at + BLK, nxt:nxt + BLK]), split(work[at:at + BLK, 0:at]), TN
                )
            work[nxt:nxt + BLK, at:nxt] = -dot3(split(work[at:at + BLK, nxt:nxt + BLK]), split(f), TN)
    ortho(RANK // wide - 1)
    store(ortho_ref, ortho_hbm, ortho_sem)
    for copy in stores:
        copy.wait()


def inverse_factor(place, projected, full):
    rows = projected.shape[0]
    tall = full.shape[1]
    hbm = pl.BlockSpec(memory_space=pltpu.HBM)
    flat, narrow, square = (rows, RANK), (rows, tall), (RANK, RANK)
    sem = pltpu.SemaphoreType.DMA
    return pl.pallas_call(
        inverse_kernel,
        out_shape=[
            jax.ShapeDtypeStruct(square, jnp.float32),
            jax.ShapeDtypeStruct((tall, RANK), jnp.float32),
            jax.ShapeDtypeStruct((rows // SIDE, RANK), jnp.float32),
        ],
        in_specs=[pl.BlockSpec(memory_space=pltpu.SMEM), hbm, hbm],
        out_specs=[hbm, hbm, hbm],
        scratch_shapes=[
            pltpu.VMEM(flat, jnp.float32), pltpu.VMEM(narrow, jnp.float32),
            pltpu.VMEM(square, jnp.float32), pltpu.VMEM((tall, RANK), jnp.float32),
            pltpu.VMEM((rows // SIDE, RANK), jnp.float32), pltpu.VMEM(square, jnp.float32),
            pltpu.VMEM(flat, jnp.bfloat16), pltpu.VMEM(flat, jnp.bfloat16),
            pltpu.VMEM(narrow, jnp.bfloat16), pltpu.VMEM(narrow, jnp.bfloat16),
            sem((SIDE,)), sem(()), sem((RANK // BLK,)), sem(()), sem(()),
        ],
        compiler_params=pltpu.CompilerParams(vmem_limit_bytes=52 * 2**20),
        cost_estimate=pl.CostEstimate(flops=60 * 10**9, bytes_accessed=18 * 2**20, transcendentals=0),
        name="inverse_factor",
    )(place, projected, full)


def place():
    col = lax.axis_index("col")
    return lax.axis_index("row"), col // (2 * SIDE), lax.rem(col // 2, SIDE), lax.rem(col, 2)


def ring(at, step):
    return lax.rem(at + step, SIDE)


def device(z, x, y, core):
    return (z, (x * SIDE + y) * 2 + core)


def greet(peers):
    barrier = pltpu.get_barrier_semaphore()
    for peer in peers:
        pl.semaphore_signal(barrier, inc=1, device_id=peer, device_id_type=MESH)
    pl.semaphore_wait(barrier, len(peers))


def remote(src, dst, send, recv, to):
    return pltpu.make_async_remote_copy(
        src_ref=src, dst_ref=dst, send_sem=send, recv_sem=recv, device_id=to, device_id_type=MESH
    )


def window_start(at):
    return at * SHARE // BLK * BLK


def gather_kernel(part_ref, buffer_ref, hbm_ref, rows_ref, out_ref, paired, total, far, near, sums, slots2, relay, *sems):
    (pair_s, pair_r, far_s, far_r, near_s, near_r, rs2_s, rs2_r, z_s, z_r, in_s, in_r, out_s, out_r,
     fwd_s, fwd_r, hop_s, hop_r, pass_s, pass_r, give_s, give_r, keep) = sems
    z, x, y, core = place()
    lanes_of = (pl.ds(0, HALF), pl.ds(HALF, HALF))
    outer = (x, y)
    inner = (y, x)

    def outer_peer(h, step):
        return device(z, ring(x, step), y, core) if h == 0 else device(z, x, ring(y, step), core)

    def inner_peer(h, step):
        return outer_peer(1 - h, step)

    turn = (1, SIDE - 1)
    twin = device(z, x, y, 1 - core)
    sides = [outer_peer(h, step) for h in range(2) for step in range(1, SIDE)]
    stack = [device(ring(z, step), x, y, core) for step in range(1, SIDE)]
    greet([twin] + sides + stack)
    sent = []

    def push(*args):
        copy = remote(*args)
        copy.start()
        sent.append(copy)
        return copy

    swap = push(part_ref.at[1 - core], paired, pair_s, pair_r, twin)

    slab_rows, window = buffer_ref.shape[0], rows_ref.shape[1]
    part = slab_rows // 2

    def columns(to, side):
        return buffer_ref.at[pl.ds(side * part, part), pl.ds(pl.multiple_of(window_start(to), BLK), window)]

    hops = []
    for side in range(2):
        hops.append(
            push(columns(ring(z, 2), side), relay.at[side], hop_s.at[side, 0], hop_r.at[side, 0], stack[turn[side] - 1])
        )

    def landing(slab, side):
        return rows_ref.at[pl.ds(pl.multiple_of(slab * slab_rows + side * part, part), part), :]

    swap.wait_recv()
    total[...] = part_ref[core] + paired[...]
    half_rows = (pl.ds(0, 32), pl.ds(32, 32))
    first, early = {}, {}
    for h in range(2):
        for side in range(2):
            first[h, side] = push(
                total.at[ring(outer[h], 2), half_rows[side], lanes_of[h]], far.at[h, side],
                far_s.at[h, side], far_r.at[h, side], outer_peer(h, turn[side]),
            )
        for side in range(2):
            early[h, side] = push(
                total.at[ring(outer[h], turn[side]), half_rows[1 - side], lanes_of[h]], near.at[h, side, half_rows[1 - side]],
                near_s.at[h, side, 0], near_r.at[h, side, 0], outer_peer(h, turn[side]),
            )
    late = {}
    for h in range(2):
        for side in range(2):
            first[h, side].wait_recv()
            block = ring(outer[h], turn[side])
            total[block, 32 * side:32 * side + 32, h * HALF:(h + 1) * HALF] += far[h, side]
            late[h, side] = push(
                total.at[block, half_rows[side], lanes_of[h]], near.at[h, side, half_rows[side]],
                near_s.at[h, side, 1], near_r.at[h, side, 1], outer_peer(h, turn[side]),
            )
    second = [[None] * 3, [None] * 3]
    for h in range(2):
        for side in range(2):
            early[h, side].wait_recv()
            late[h, side].wait_recv()
        summed = total[outer[h], :, h * HALF:(h + 1) * HALF] + near[h, 0] + near[h, 1]
        sums[h] = summed.reshape(SIDE, 16, HALF)
        for step in (2, 1, 3):
            second[h][step - 1] = push(
                sums.at[h, ring(inner[h], step)], slots2.at[h, step - 1],
                rs2_s.at[h, step - 1], rs2_r.at[h, step - 1], inner_peer(h, step),
            )

    up = [[None] * 3, [None] * 3]
    for h in range(2):
        for copy in second[h]:
            copy.wait_recv()
        done = sums[h, inner[h]] + slots2[h, 0] + slots2[h, 1] + slots2[h, 2]
        out_ref[z, core, outer[h], inner[h], :, h * HALF:(h + 1) * HALF] = done
        own = out_ref.at[z, core, outer[h], inner[h], :, lanes_of[h]]
        for step in (2, 1, 3):
            up[h][step - 1] = push(own, own, z_s.at[h, step - 1], z_r.at[h, step - 1], stack[step - 1])

    rows_ref[pl.ds(pl.multiple_of(z * slab_rows, slab_rows), slab_rows), :] = buffer_ref[
        :, pl.ds(pl.multiple_of(window_start(z), BLK), window)
    ]

    def spread(h, at, peer, ref_of, cuts, send, recv, fwd_send, fwd_recv):
        count = len(cuts)
        order = (list(range(count)), list(range(count // 2, count)) + list(range(count // 2)))
        copies, passed = {}, {}
        for k in range(count):
            for side in range(2):
                cut = order[side][k]
                ref = ref_of(cuts[cut], at)
                copies[side, cut] = push(ref, ref, send.at[h, side, cut], recv.at[h, side, cut], peer(h, turn[side]))

        def relay_on(k):
            for side in range(2):
                cut = order[side][k]
                copies[side, cut].wait_recv()
                ref = ref_of(cuts[cut], ring(at, turn[1 - side]))
                passed[cut] = push(ref, ref, fwd_send.at[h, cut], fwd_recv.at[h, cut], peer(h, turn[side]))

        def wait_side(side):
            for k in range(count // 2, count):
                copies[side, order[side][k]].wait_recv()

        def wait_passed():
            for cut in range(count):
                passed[cut].wait_recv()

        return relay_on, wait_side, wait_passed

    back = []
    for h in range(2):
        for copy in up[h]:
            copy.wait_recv()

        def strip(cut, at, h=h):
            return out_ref.at[cut, core, outer[h], at, :, lanes_of[h]]

        back.append(spread(h, inner[h], inner_peer, strip, (pl.ds(0, 2), pl.ds(2, 2)), in_s, in_r, pass_s, pass_r))
    for side in range(2):
        hops[side].wait_recv()
        ref = relay.at[side]
        hops.append(
            push(ref, landing(ring(z, turn[1 - side]), side), hop_s.at[side, 1], hop_r.at[side, 1], stack[turn[side] - 1])
        )
        for half in range(2):
            hops.append(
                push(
                    columns(ring(z, turn[side]), half), landing(z, half),
                    hop_s.at[side, 2 + half], hop_r.at[side, 2 + half], stack[turn[side] - 1],
                )
            )
    for h in range(2):
        back[h][0](0)

    def give(h, group, at):
        ref = out_ref.at[:, core, group, :, :, lanes_of[h]]
        return push(ref, ref, give_s.at[h, at], give_r.at[h, at], twin)

    ahead, got = [], []
    for h in range(2):
        for side in range(2):
            back[h][1](side)
        back[h][2]()

        def block(cut, at, h=h):
            return out_ref.at[cut, core, at, :, :, lanes_of[h]]

        ahead.append(spread(h, outer[h], outer_peer, block, tuple(range(SIDE)), out_s, out_r, fwd_s, fwd_r))
    for h in range(2):
        got.append(give(h, outer[h], 0))
    for k in range(2):
        for h in range(2):
            ahead[h][0](k)
    for h in range(2):
        for side in range(2):
            ahead[h][1](side)
            got.append(give(h, ring(outer[h], turn[1 - side]), 1 + side))
    for h in range(2):
        ahead[h][2]()
        got.append(give(h, ring(outer[h], 2), 3))
    for copy in got + hops[2:]:
        copy.wait_recv()
    store = pltpu.make_async_copy(out_ref, hbm_ref, keep)
    store.start()
    for copy in sent:
        copy.wait_send()
    store.wait()


def gather_projected(part, buffer):
    rows = part.shape[0]
    sem = pltpu.SemaphoreType.DMA
    pair = lambda *shape: [sem(shape), sem(shape)]
    vmem = pl.BlockSpec(memory_space=pltpu.VMEM)
    full = (SIDE, 2, SIDE, SIDE, 16, RANK)
    out, columns = pl.pallas_call(
        gather_kernel,
        out_shape=[
            jax.ShapeDtypeStruct(full, jnp.float32),
            jax.ShapeDtypeStruct((SIDE * rows, WINDOW), jnp.float32),
        ],
        in_specs=[vmem, vmem],
        out_specs=[pl.BlockSpec(memory_space=pltpu.HBM), vmem],
        scratch_shapes=[
            pltpu.VMEM(full, jnp.float32),
            pltpu.VMEM((SIDE, 64, RANK), jnp.float32),
            pltpu.VMEM((SIDE, 64, RANK), jnp.float32),
            pltpu.VMEM((2, 2, 32, HALF), jnp.float32),
            pltpu.VMEM((2, 2, 64, HALF), jnp.float32),
            pltpu.VMEM((2, SIDE, 16, HALF), jnp.float32),
            pltpu.VMEM((2, 3, 16, HALF), jnp.float32),
            pltpu.VMEM((2, rows // 2, WINDOW), jnp.float32),
            *pair(), *pair(2, 2), *pair(2, 2, 2), *pair(2, 3), *pair(2, 3), *pair(2, 2, 2), *pair(2, 2, SIDE),
            *pair(2, SIDE), *pair(2, SIDE), *pair(2, 2), *pair(2, SIDE), sem(()),
        ],
        compiler_params=pltpu.CompilerParams(collective_id=0, has_side_effects=True, vmem_limit_bytes=52 * 2**20),
        cost_estimate=pl.CostEstimate(flops=10**6, bytes_accessed=12 * 2**20, transcendentals=0),
        name="gather_projected",
    )(part.reshape(2, SIDE, 64, RANK), buffer)
    return out.reshape(SIDE * rows, RANK), columns


def norm_kernel(part_ref, out_ref, held, slots, pair_s, pair_r, one_s, one_r, two_s, two_r):
    z, x, y, core = place()
    twin = device(z, x, y, 1 - core)
    along_x = [device(z, ring(x, step), y, core) for step in range(1, SIDE)]
    along_y = [device(z, x, ring(y, step), core) for step in range(1, SIDE)]
    greet([twin] + along_x + along_y)
    swap = remote(part_ref, slots.at[0], pair_s, pair_r, twin)
    swap.start()
    swap.wait()
    held[0] = part_ref[...] + slots[0]
    for turn, (peers, send, recv) in enumerate(((along_x, one_s, one_r), (along_y, two_s, two_r))):
        copies = []
        for step in range(3):
            copy = remote(held.at[turn], slots.at[1 + 3 * turn + step], send.at[step], recv.at[step], peers[step])
            copy.start()
            copies.append(copy)
        for copy in copies:
            copy.wait()
        summed = held[turn] + slots[1 + 3 * turn] + slots[2 + 3 * turn] + slots[3 + 3 * turn]
        if turn == 0:
            held[1] = summed
        else:
            out_ref[...] = summed


def sum_norms(part):
    sem = pltpu.SemaphoreType.DMA
    tile = (8, BLK)
    out = pl.pallas_call(
        norm_kernel,
        out_shape=jax.ShapeDtypeStruct(tile, jnp.float32),
        in_specs=[pl.BlockSpec(memory_space=pltpu.VMEM)],
        out_specs=pl.BlockSpec(memory_space=pltpu.VMEM),
        scratch_shapes=[
            pltpu.VMEM((2,) + tile, jnp.float32),
            pltpu.VMEM((7,) + tile, jnp.float32),
            sem(()), sem(()), sem((3,)), sem((3,)), sem((3,)), sem((3,)),
        ],
        compiler_params=pltpu.CompilerParams(collective_id=1, has_side_effects=True, vmem_limit_bytes=2 * 2**20),
        name="sum_norms",
    )(part.reshape(tile))
    return out.reshape(RANK)


def apply_kernel(spread, own, inverse, right_hbm, square_ref, mixed, stage, right, hi, lo, in_sem, inv_sem, out_sem):
    tall, share = own.shape[0], spread.shape[0] // SIDE
    pieces = [(own, 0, spread.shape[0], tall)] + [(spread, i * share, i * share, share) for i in range(SIDE)]
    load = pltpu.make_async_copy(inverse, stage, inv_sem)
    load.start()
    loads, stores = [], []
    for i, (src, first, at, rows) in enumerate(pieces):
        loads.append(pltpu.make_async_copy(src.at[pl.ds(first, rows)], mixed.at[pl.ds(at, rows)], in_sem.at[i]))
        loads[-1].start()
    load.wait()
    hi[...], lo[...] = split(stage[...])
    for i, (_, _, at, rows) in enumerate(pieces):
        loads[i].wait()
        left = split(mixed[at:at + rows, :])
        for c in range(0, RANK, 256):
            deep = c + 256
            weight = (hi[c:deep, :deep], lo[c:deep, :deep])
            got = dot3((left[0][:, :deep], left[1][:, :deep]), weight, NT)
            right[at:at + rows, c:deep] = got
            squares = jnp.sum((got * got).reshape(-1, 8, 256), axis=0)
            square_ref[:, c:deep] = squares if i == 0 else square_ref[:, c:deep] + squares
        stores.append(pltpu.make_async_copy(right.at[pl.ds(at, rows)], right_hbm.at[pl.ds(at, rows)], out_sem.at[i]))
        stores[-1].start()
    for copy in stores:
        copy.wait()


def apply_inverse(spread, own, inverse):
    shape = (spread.shape[0] + own.shape[0], RANK)
    square = (RANK, RANK)
    hbm = pl.BlockSpec(memory_space=pltpu.HBM)
    sem = pltpu.SemaphoreType.DMA
    return pl.pallas_call(
        apply_kernel,
        out_shape=[jax.ShapeDtypeStruct(shape, jnp.float32), jax.ShapeDtypeStruct((8, RANK), jnp.float32)],
        in_specs=[hbm, hbm, hbm],
        out_specs=[hbm, pl.BlockSpec(memory_space=pltpu.VMEM)],
        scratch_shapes=[
            pltpu.VMEM(shape, jnp.float32), pltpu.VMEM(square, jnp.float32), pltpu.VMEM(shape, jnp.float32),
            pltpu.VMEM(square, jnp.bfloat16), pltpu.VMEM(square, jnp.bfloat16),
            sem((SIDE + 1,)), sem(()), sem((SIDE + 1,)),
        ],
        compiler_params=pltpu.CompilerParams(vmem_limit_bytes=58 * 2**20),
        cost_estimate=pl.CostEstimate(flops=8 * 10**9, bytes_accessed=18 * 2**20, transcendentals=0),
        name="apply_inverse",
    )(spread, own, inverse)


def dot(a, b, contract, precision):
    return lax.dot_general(a, b, (contract, ((), ())), precision=precision, preferred_element_type=jnp.float32)


def body(momentum, gradient, basis):
    total_cols = basis.shape[0] * lax.axis_size("col")
    buffer = momentum + gradient.astype(jnp.float32)
    place_z = lax.axis_index("row").astype(jnp.int32)
    full = lax.all_gather(buffer[:, SIDE * SHARE:], "row", axis=0, tiled=True)
    local_proj = dot(buffer, basis, NN, high)
    projected, columns = gather_projected(local_proj, buffer)
    mixed = dot(columns, projected, TN, high)
    mixed = lax.dynamic_slice_in_dim(mixed, place_z * SHARE - window_start(place_z), SHARE, 0)
    spread = lax.all_gather(mixed, "row", axis=0, tiled=True)
    inverse, own, orthonormal = inverse_factor(place_z.reshape(1), projected, full)
    right_factor, squares = apply_inverse(spread, own, inverse)
    squares = sum_norms(jnp.sum(squares, axis=0))
    col_scale = jnp.sqrt(squares / total_cols + 1e-06)
    new_basis = right_factor / col_scale[None, :]
    feedback = dot(orthonormal, right_factor, NT, lax.Precision.DEFAULT)
    new_momentum = buffer - 0.05 * feedback
    update = dot(orthonormal, new_basis, NT, high)
    return (new_momentum, new_basis, update.astype(jnp.bfloat16))


def solution(mesh):
    in_specs = (P("row", "col"), P("row", "col"), P("col", None))
    out_specs = (P("row", "col"), P("col", None), P("row", "col"))
    return jax.shard_map(body, mesh=mesh, in_specs=in_specs, out_specs=out_specs, check_vma=False)
```

```python
import functools
import jax
import jax.numpy as jnp
from jax import lax
from jax.experimental import pallas as pl
from jax.experimental.pallas import tpu as pltpu
from jax.sharding import PartitionSpec as P

highest = lax.Precision.HIGHEST
high = lax.Precision.HIGH
MESH = pl.DeviceIdType.MESH
RANK = 1024
BLK = 128
BASE = 32
SIDE = 4
HALF = RANK // 2
SHARE = 416
WINDOW = 512


def dot_tn(a, b):
    return lax.dot_general(a, b, (((0,), (0,)), ((), ())), precision=highest, preferred_element_type=jnp.float32)

def dot_nn(a, b):
    return lax.dot_general(a, b, (((1,), (0,)), ((), ())), precision=highest, preferred_element_type=jnp.float32)

def lanes(col):
    return jnp.broadcast_to(col, (8, BLK))

def eliminate(tiles, off, fill):
    lane = lax.broadcasted_iota(jnp.int32, (8, BLK), 1)
    sub = lax.broadcasted_iota(jnp.int32, (8, BLK), 0)
    n = len(tiles)
    done = []
    for g in range(n):
        first = off + 8 * g
        cols = [[lanes(tiles[t][:, first + j:first + j + 1]) for j in range(8)] for t in range(g, n)]
        inside = (lane >= first) & (lane < first + 8)
        tiles[g] = jnp.where(inside, jnp.where(lane - first == sub, 1.0, 0.0), tiles[g])
        for t in range(g + 1, n):
            tiles[t] = jnp.where(inside, 0.0, tiles[t])
        el = [[jnp.broadcast_to(cols[0][j][i:i + 1, :], (8, BLK)) if j >= i else None for j in range(8)] for i in range(8)]
        scale = jnp.zeros((8, BLK), jnp.float32)
        for i in range(8):
            rinv = pl.reciprocal(el[i][i], approx=True)
            rinv = rinv * (2.0 - el[i][i] * rinv)
            scale = jnp.where(sub == i, el[i][i], scale)
            mult = [None] * 8
            for j in range(i + 1, 8):
                mult[j] = el[i][j] * rinv
                for l in range(j, 8):
                    el[j][l] = el[j][l] - mult[j] * el[i][l]
            row = jnp.broadcast_to(tiles[g][i:i + 1, :], (8, BLK)) * rinv
            for t in range(g, n):
                c = cols[t - g][i]
                for j in range(i + 1, 8):
                    cols[t - g][j] = cols[t - g][j] - c * mult[j]
                if t == g:
                    c = jnp.where(sub > i, c, 0.0)
                tiles[t] = tiles[t] - c * row
        done.append(tiles[g] * lax.rsqrt(scale))
        fill()
    full = jnp.concatenate(done, axis=0)
    ln = lax.broadcasted_iota(jnp.int32, full.shape, 1) - off
    rw = lax.broadcasted_iota(jnp.int32, full.shape, 0)
    return jnp.where((ln > rw) & (ln < 8 * n), 0.0, full)

def invert_block(work, at, fill):
    lane = lax.broadcasted_iota(jnp.int32, (BLK, BLK), 1)
    blk = work[pl.ds(at, BLK), pl.ds(at, BLK)]
    parts = []
    for b in range(BLK // BASE):
        lo = b * BASE
        rows = blk[0:BASE, :]
        tiles = [rows[8 * t:8 * t + 8, :] for t in range(BASE // 8)]
        s = eliminate(tiles, lo, fill)
        parts.append(s)
        if lo + BASE < BLK:
            upd = dot_tn(s, s)
            rest = blk[BASE:, :]
            ln = lax.broadcasted_iota(jnp.int32, rest.shape, 1)
            blk = jnp.where((ln >= lo) & (ln < lo + BASE), 0.0, rest) - upd[lo + BASE:, :]
    f = jnp.concatenate(parts, axis=0)
    row = lax.broadcasted_iota(jnp.int32, (BLK, BLK), 0)
    return jnp.where(row >= lane, f, 0.0)


NN = ((1,), (0,))
NT = ((1,), (1,))


def split(x):
    hi = x.astype(jnp.bfloat16)
    return hi, (x - hi.astype(jnp.float32)).astype(jnp.bfloat16)


def dot3(a, b, contract):
    one = functools.partial(
        lax.dot_general, dimension_numbers=(contract, ((), ())), preferred_element_type=jnp.float32
    )
    return one(a[0], b[0]) + (one(a[0], b[1]) + one(a[1], b[0]))

TN = ((0,), (0,))


def inverse_kernel(place_ref, proj_hbm, out_hbm, ortho_hbm, proj_ref, out_ref, ortho_ref, work, hi, lo_part,
                   proj_sem, out_sem, ortho_sem):
    nb = RANK // BLK
    wide = 2 * BLK
    queue = []

    def fill():
        if queue:
            queue.pop(0)()

    def gram(pair, col):
        rows, cols = slice(pair * wide, pair * wide + wide), slice(col * wide, col * wide + wide)
        work[rows, cols] = dot3((hi[:, rows], lo_part[:, rows]), (hi[:, cols], lo_part[:, cols]), TN)

    def right(i, first, last, lo, up):
        at = i * BLK
        left = slice(first * BLK, last * BLK)
        work[at:at + BLK, lo:up] -= dot_tn(work[left, at:at + BLK], work[left, lo:up])

    def left(i, c, last):
        at, lo = i * BLK, c * BLK
        rows = slice(lo, last * BLK)
        work[at:at + BLK, lo:lo + BLK] = -dot3(split(work[rows, at:at + BLK]), split(work[rows, lo:lo + BLK]), TN)

    def ortho(pair):
        cols = slice(pair * wide, pair * wide + wide)
        mine = pl.ds(pl.multiple_of(place_ref[0] * ortho_ref.shape[0], 512), ortho_ref.shape[0])
        deep = pair * wide + wide
        ortho_ref[:, cols] = dot3((hi[mine, :deep], lo_part[mine, :deep]), split(out_ref[cols, :deep]), NT)

    def later(f, *args):
        queue.append(functools.partial(f, *args))

    stores = []

    def store(src, dst, sem):
        copy = pltpu.make_async_copy(src, dst, sem)
        copy.start()
        stores.append(copy)

    chunk = proj_ref.shape[0] // SIDE
    loads = [
        pltpu.make_async_copy(proj_hbm.at[pl.ds(i * chunk, chunk)], proj_ref.at[pl.ds(i * chunk, chunk)], proj_sem.at[i])
        for i in range(SIDE)
    ]
    for copy in loads:
        copy.start()
    for i in range(SIDE):
        loads[i].wait()
        part = slice(i * chunk, i * chunk + chunk)
        hi[part, :], lo_part[part, :] = split(proj_ref[part, :])
    for col in range(RANK // wide):
        gram(0, col)
    for j in range(nb):
        at = j * BLK
        if j % 2 == 0 and j + 2 < nb:
            for col in range(j // 2 + 1, RANK // wide):
                later(gram, j // 2 + 1, col)
        if j and j + 1 < nb:
            for lo in range(at + BLK, RANK, wide):
                later(right, j + 1, 0, j, lo, min(lo + wide, RANK))
            for c in range(j):
                later(left, j + 1, c, j)
        if j and j % 2 == 0:
            later(ortho, j // 2 - 1)
        f = invert_block(work, at, fill)
        while queue:
            fill()
        if at:
            work[at:at + BLK, 0:at] = dot3(split(f), split(work[at:at + BLK, 0:at]), NN)
        if j + 1 < nb:
            work[at:at + BLK, at + BLK:] = dot_nn(f, work[at:at + BLK, at + BLK:])
        work[at:at + BLK, at:at + BLK] = f
        out_ref[at:at + BLK, 0:at + BLK] = work[at:at + BLK, 0:at + BLK]
        if j + 1 == nb:
            store(out_ref.at[pl.ds(at, BLK)], out_hbm.at[pl.ds(at, BLK)], out_sem.at[j])
        if j + 1 < nb:
            out_ref[at:at + BLK, at + BLK:] = jnp.zeros((BLK, RANK - at - BLK), jnp.float32)
            store(out_ref.at[pl.ds(at, BLK)], out_hbm.at[pl.ds(at, BLK)], out_sem.at[j])
            right(j + 1, j, j + 1, at + BLK, RANK)
            nxt = at + BLK
            if at:
                work[nxt:nxt + BLK, 0:at] -= dot3(
                    split(work[at:at + BLK, nxt:nxt + BLK]), split(work[at:at + BLK, 0:at]), TN
                )
            work[nxt:nxt + BLK, at:nxt] = -dot3(split(work[at:at + BLK, nxt:nxt + BLK]), split(f), TN)
    ortho(RANK // wide - 1)
    store(ortho_ref, ortho_hbm, ortho_sem)
    for copy in stores:
        copy.wait()


def inverse_factor(place, projected):
    rows = projected.shape[0]
    hbm = pl.BlockSpec(memory_space=pltpu.HBM)
    flat, square = (rows, RANK), (RANK, RANK)
    sem = pltpu.SemaphoreType.DMA
    return pl.pallas_call(
        inverse_kernel,
        out_shape=[
            jax.ShapeDtypeStruct(square, jnp.float32),
            jax.ShapeDtypeStruct((rows // SIDE, RANK), jnp.float32),
        ],
        in_specs=[pl.BlockSpec(memory_space=pltpu.SMEM), hbm],
        out_specs=[hbm, hbm],
        scratch_shapes=[
            pltpu.VMEM(flat, jnp.float32), pltpu.VMEM(square, jnp.float32),
            pltpu.VMEM((rows // SIDE, RANK), jnp.float32), pltpu.VMEM(square, jnp.float32),
            pltpu.VMEM(flat, jnp.bfloat16), pltpu.VMEM(flat, jnp.bfloat16),
            sem((SIDE,)), sem((RANK // BLK,)), sem(()),
        ],
        compiler_params=pltpu.CompilerParams(vmem_limit_bytes=52 * 2**20),
        cost_estimate=pl.CostEstimate(flops=60 * 10**9, bytes_accessed=18 * 2**20, transcendentals=0),
        name="inverse_factor",
    )(place, projected)


def place():
    col = lax.axis_index("col")
    return lax.axis_index("row"), col // (2 * SIDE), lax.rem(col // 2, SIDE), lax.rem(col, 2)


def ring(at, step):
    return lax.rem(at + step, SIDE)


def device(z, x, y, core):
    return (z, (x * SIDE + y) * 2 + core)


def greet(peers):
    barrier = pltpu.get_barrier_semaphore()
    for peer in peers:
        pl.semaphore_signal(barrier, inc=1, device_id=peer, device_id_type=MESH)
    pl.semaphore_wait(barrier, len(peers))


def remote(src, dst, send, recv, to):
    return pltpu.make_async_remote_copy(
        src_ref=src, dst_ref=dst, send_sem=send, recv_sem=recv, device_id=to, device_id_type=MESH
    )


def window_start(at):
    return at * SHARE // BLK * BLK


def gather_kernel(part_ref, buffer_ref, hbm_ref, rows_ref, out_ref, paired, total, far, near, sums, slots2, relay, *sems):
    (pair_s, pair_r, far_s, far_r, near_s, near_r, rs2_s, rs2_r, z_s, z_r, in_s, in_r, out_s, out_r,
     fwd_s, fwd_r, hop_s, hop_r, pass_s, pass_r, give_s, give_r, keep) = sems
    z, x, y, core = place()
    lanes_of = (pl.ds(0, HALF), pl.ds(HALF, HALF))
    outer = (x, y)
    inner = (y, x)

    def outer_peer(h, step):
        return device(z, ring(x, step), y, core) if h == 0 else device(z, x, ring(y, step), core)

    def inner_peer(h, step):
        return outer_peer(1 - h, step)

    turn = (1, SIDE - 1)
    twin = device(z, x, y, 1 - core)
    sides = [outer_peer(h, step) for h in range(2) for step in range(1, SIDE)]
    stack = [device(ring(z, step), x, y, core) for step in range(1, SIDE)]
    greet([twin] + sides + stack)
    sent = []

    def push(*args):
        copy = remote(*args)
        copy.start()
        sent.append(copy)
        return copy

    swap = push(part_ref.at[1 - core], paired, pair_s, pair_r, twin)

    slab_rows, window = buffer_ref.shape[0], rows_ref.shape[1]
    part = slab_rows // 2

    def columns(to, side):
        return buffer_ref.at[pl.ds(side * part, part), pl.ds(pl.multiple_of(window_start(to), BLK), window)]

    hops = []
    for side in range(2):
        hops.append(
            push(columns(ring(z, 2), side), relay.at[side], hop_s.at[side, 0], hop_r.at[side, 0], stack[turn[side] - 1])
        )

    def landing(slab, side):
        return rows_ref.at[pl.ds(pl.multiple_of(slab * slab_rows + side * part, part), part), :]

    swap.wait_recv()
    total[...] = part_ref[core] + paired[...]
    half_rows = (pl.ds(0, 32), pl.ds(32, 32))
    first, early = {}, {}
    for h in range(2):
        for side in range(2):
            first[h, side] = push(
                total.at[ring(outer[h], 2), half_rows[side], lanes_of[h]], far.at[h, side],
                far_s.at[h, side], far_r.at[h, side], outer_peer(h, turn[side]),
            )
        for side in range(2):
            early[h, side] = push(
                total.at[ring(outer[h], turn[side]), half_rows[1 - side], lanes_of[h]], near.at[h, side, half_rows[1 - side]],
                near_s.at[h, side, 0], near_r.at[h, side, 0], outer_peer(h, turn[side]),
            )
    late = {}
    for h in range(2):
        for side in range(2):
            first[h, side].wait_recv()
            block = ring(outer[h], turn[side])
            total[block, 32 * side:32 * side + 32, h * HALF:(h + 1) * HALF] += far[h, side]
            late[h, side] = push(
                total.at[block, half_rows[side], lanes_of[h]], near.at[h, side, half_rows[side]],
                near_s.at[h, side, 1], near_r.at[h, side, 1], outer_peer(h, turn[side]),
            )
    second = [[None] * 3, [None] * 3]
    for h in range(2):
        for side in range(2):
            early[h, side].wait_recv()
            late[h, side].wait_recv()
        summed = total[outer[h], :, h * HALF:(h + 1) * HALF] + near[h, 0] + near[h, 1]
        sums[h] = summed.reshape(SIDE, 16, HALF)
        for step in (2, 1, 3):
            second[h][step - 1] = push(
                sums.at[h, ring(inner[h], step)], slots2.at[h, step - 1],
                rs2_s.at[h, step - 1], rs2_r.at[h, step - 1], inner_peer(h, step),
            )

    up = [[None] * 3, [None] * 3]
    for h in range(2):
        for copy in second[h]:
            copy.wait_recv()
        done = sums[h, inner[h]] + slots2[h, 0] + slots2[h, 1] + slots2[h, 2]
        out_ref[z, core, outer[h], inner[h], :, h * HALF:(h + 1) * HALF] = done
        own = out_ref.at[z, core, outer[h], inner[h], :, lanes_of[h]]
        for step in (2, 1, 3):
            up[h][step - 1] = push(own, own, z_s.at[h, step - 1], z_r.at[h, step - 1], stack[step - 1])

    rows_ref[pl.ds(pl.multiple_of(z * slab_rows, slab_rows), slab_rows), :] = buffer_ref[
        :, pl.ds(pl.multiple_of(window_start(z), BLK), window)
    ]

    def spread(h, at, peer, ref_of, cuts, send, recv, fwd_send, fwd_recv):
        count = len(cuts)
        order = (list(range(count)), list(range(count // 2, count)) + list(range(count // 2)))
        copies, passed = {}, {}
        for k in range(count):
            for side in range(2):
                cut = order[side][k]
                ref = ref_of(cuts[cut], at)
                copies[side, cut] = push(ref, ref, send.at[h, side, cut], recv.at[h, side, cut], peer(h, turn[side]))

        def relay_on(k):
            for side in range(2):
                cut = order[side][k]
                copies[side, cut].wait_recv()
                ref = ref_of(cuts[cut], ring(at, turn[1 - side]))
                passed[cut] = push(ref, ref, fwd_send.at[h, cut], fwd_recv.at[h, cut], peer(h, turn[side]))

        def wait_side(side):
            for k in range(count // 2, count):
                copies[side, order[side][k]].wait_recv()

        def wait_passed():
            for cut in range(count):
                passed[cut].wait_recv()

        return relay_on, wait_side, wait_passed

    back = []
    for h in range(2):
        for copy in up[h]:
            copy.wait_recv()

        def strip(cut, at, h=h):
            return out_ref.at[cut, core, outer[h], at, :, lanes_of[h]]

        back.append(spread(h, inner[h], inner_peer, strip, (pl.ds(0, 2), pl.ds(2, 2)), in_s, in_r, pass_s, pass_r))
    for side in range(2):
        hops[side].wait_recv()
        ref = relay.at[side]
        hops.append(
            push(ref, landing(ring(z, turn[1 - side]), side), hop_s.at[side, 1], hop_r.at[side, 1], stack[turn[side] - 1])
        )
        for half in range(2):
            hops.append(
                push(
                    columns(ring(z, turn[side]), half), landing(z, half),
                    hop_s.at[side, 2 + half], hop_r.at[side, 2 + half], stack[turn[side] - 1],
                )
            )
    for h in range(2):
        back[h][0](0)

    def give(h, group, at):
        ref = out_ref.at[:, core, group, :, :, lanes_of[h]]
        return push(ref, ref, give_s.at[h, at], give_r.at[h, at], twin)

    ahead, got = [], []
    for h in range(2):
        for side in range(2):
            back[h][1](side)
        back[h][2]()

        def block(cut, at, h=h):
            return out_ref.at[cut, core, at, :, :, lanes_of[h]]

        ahead.append(spread(h, outer[h], outer_peer, block, tuple(range(SIDE)), out_s, out_r, fwd_s, fwd_r))
    for h in range(2):
        got.append(give(h, outer[h], 0))
    for k in range(2):
        for h in range(2):
            ahead[h][0](k)
    for h in range(2):
        for side in range(2):
            ahead[h][1](side)
            got.append(give(h, ring(outer[h], turn[1 - side]), 1 + side))
    for h in range(2):
        ahead[h][2]()
        got.append(give(h, ring(outer[h], 2), 3))
    for copy in got + hops[2:]:
        copy.wait_recv()
    store = pltpu.make_async_copy(out_ref, hbm_ref, keep)
    store.start()
    for copy in sent:
        copy.wait_send()
    store.wait()


def gather_projected(part, buffer):
    rows = part.shape[0]
    sem = pltpu.SemaphoreType.DMA
    pair = lambda *shape: [sem(shape), sem(shape)]
    vmem = pl.BlockSpec(memory_space=pltpu.VMEM)
    full = (SIDE, 2, SIDE, SIDE, 16, RANK)
    out, columns = pl.pallas_call(
        gather_kernel,
        out_shape=[
            jax.ShapeDtypeStruct(full, jnp.float32),
            jax.ShapeDtypeStruct((SIDE * rows, WINDOW), jnp.float32),
        ],
        in_specs=[vmem, vmem],
        out_specs=[pl.BlockSpec(memory_space=pltpu.HBM), vmem],
        scratch_shapes=[
            pltpu.VMEM(full, jnp.float32),
            pltpu.VMEM((SIDE, 64, RANK), jnp.float32),
            pltpu.VMEM((SIDE, 64, RANK), jnp.float32),
            pltpu.VMEM((2, 2, 32, HALF), jnp.float32),
            pltpu.VMEM((2, 2, 64, HALF), jnp.float32),
            pltpu.VMEM((2, SIDE, 16, HALF), jnp.float32),
            pltpu.VMEM((2, 3, 16, HALF), jnp.float32),
            pltpu.VMEM((2, rows // 2, WINDOW), jnp.float32),
            *pair(), *pair(2, 2), *pair(2, 2, 2), *pair(2, 3), *pair(2, 3), *pair(2, 2, 2), *pair(2, 2, SIDE),
            *pair(2, SIDE), *pair(2, SIDE), *pair(2, 2), *pair(2, SIDE), sem(()),
        ],
        compiler_params=pltpu.CompilerParams(collective_id=0, has_side_effects=True, vmem_limit_bytes=52 * 2**20),
        cost_estimate=pl.CostEstimate(flops=10**6, bytes_accessed=12 * 2**20, transcendentals=0),
        name="gather_projected",
    )(part.reshape(2, SIDE, 64, RANK), buffer)
    return out.reshape(SIDE * rows, RANK), columns


def apply_kernel(mixed_hbm, inverse, right_hbm, norm_ref, mixed, stage, right, hi, lo, square, held, slots,
                 in_sem, inv_sem, out_sem, pair_s, pair_r, one_s, one_r, two_s, two_r):
    z, x, y, core = place()
    twin = device(z, x, y, 1 - core)
    along_x = [device(z, ring(x, step), y, core) for step in range(1, SIDE)]
    along_y = [device(z, x, ring(y, step), core) for step in range(1, SIDE)]
    peers = [twin] + along_x + along_y
    barrier = pltpu.get_barrier_semaphore()
    for peer in peers:
        pl.semaphore_signal(barrier, inc=1, device_id=peer, device_id_type=MESH)

    load = pltpu.make_async_copy(inverse, stage, inv_sem)
    load.start()
    rows = mixed_hbm.shape[0] // SIDE
    loads, stores = [], []
    for i in range(SIDE):
        part = pl.ds(i * rows, rows)
        loads.append(pltpu.make_async_copy(mixed_hbm.at[part], mixed.at[part], in_sem.at[i]))
        loads[-1].start()
    load.wait()
    hi[...], lo[...] = split(stage[...])
    for i in range(SIDE):
        at = i * rows
        loads[i].wait()
        left = split(mixed[at:at + rows, :])
        for c in range(0, RANK, 256):
            deep = c + 256
            weight = (hi[c:deep, :deep], lo[c:deep, :deep])
            got = dot3((left[0][:, :deep], left[1][:, :deep]), weight, NT)
            right[at:at + rows, c:deep] = got
            squares = jnp.sum((got * got).reshape(-1, 8, 256), axis=0)
            square[:, c:deep] = squares if i == 0 else square[:, c:deep] + squares
        part = pl.ds(at, rows)
        stores.append(pltpu.make_async_copy(right.at[part], right_hbm.at[part], out_sem.at[i]))
        stores[-1].start()

    held[0] = square[...]
    pl.semaphore_wait(barrier, len(peers))
    swap = remote(held.at[0], slots.at[0], pair_s, pair_r, twin)
    swap.start()
    swap.wait()
    held[1] = held[0] + slots[0]
    for turn, (others, send, recv) in enumerate(((along_x, one_s, one_r), (along_y, two_s, two_r))):
        copies = []
        for step in range(3):
            copy = remote(held.at[1 + turn], slots.at[1 + 3 * turn + step], send.at[step], recv.at[step], others[step])
            copy.start()
            copies.append(copy)
        for copy in copies:
            copy.wait()
        first = 1 + 3 * turn
        held[2 + turn] = held[1 + turn] + slots[first] + slots[first + 1] + slots[first + 2]
    norm_ref[...] = held[3]
    for copy in stores:
        copy.wait()


def apply_inverse(mixed, inverse):
    shape = mixed.shape
    square = (RANK, RANK)
    flat = (8, RANK)
    hbm = pl.BlockSpec(memory_space=pltpu.HBM)
    sem = pltpu.SemaphoreType.DMA
    return pl.pallas_call(
        apply_kernel,
        out_shape=[jax.ShapeDtypeStruct(shape, jnp.float32), jax.ShapeDtypeStruct(flat, jnp.float32)],
        in_specs=[hbm, hbm],
        out_specs=[hbm, pl.BlockSpec(memory_space=pltpu.VMEM)],
        scratch_shapes=[
            pltpu.VMEM(shape, jnp.float32), pltpu.VMEM(square, jnp.float32), pltpu.VMEM(shape, jnp.float32),
            pltpu.VMEM(square, jnp.bfloat16), pltpu.VMEM(square, jnp.bfloat16), pltpu.VMEM(flat, jnp.float32),
            pltpu.VMEM((4,) + flat, jnp.float32), pltpu.VMEM((7,) + flat, jnp.float32),
            sem((SIDE,)), sem(()), sem((SIDE,)), sem(()), sem(()), sem((3,)), sem((3,)), sem((3,)), sem((3,)),
        ],
        compiler_params=pltpu.CompilerParams(collective_id=1, has_side_effects=True, vmem_limit_bytes=58 * 2**20),
        cost_estimate=pl.CostEstimate(flops=8 * 10**9, bytes_accessed=18 * 2**20, transcendentals=0),
        name="apply_inverse",
    )(mixed, inverse)


def dot(a, b, contract, precision):
    return lax.dot_general(a, b, (contract, ((), ())), precision=precision, preferred_element_type=jnp.float32)


def body(momentum, gradient, basis):
    total_cols = basis.shape[0] * lax.axis_size("col")
    buffer = momentum + gradient.astype(jnp.float32)
    place_z = lax.axis_index("row").astype(jnp.int32)
    local_proj = dot(buffer, basis, NN, high)
    projected, columns = gather_projected(local_proj, buffer)
    mixed = dot(columns, projected, TN, high)
    mixed = lax.dynamic_slice_in_dim(mixed, place_z * SHARE - window_start(place_z), SHARE, 0)
    mixed = lax.all_gather(mixed, "row", axis=0, tiled=True)
    inverse, orthonormal = inverse_factor(place_z.reshape(1), projected)
    right_factor, squares = apply_inverse(mixed, inverse)
    squares = jnp.sum(squares, axis=0)
    col_scale = jnp.sqrt(squares / total_cols + 1e-06)
    new_basis = right_factor / col_scale[None, :]
    feedback = dot(orthonormal, right_factor, NT, lax.Precision.DEFAULT)
    new_momentum = buffer - 0.05 * feedback
    update = dot(orthonormal, new_basis, NT, high)
    return (new_momentum, new_basis, update.astype(jnp.bfloat16))


def solution(mesh):
    in_specs = (P("row", "col"), P("row", "col"), P("col", None))
    out_specs = (P("row", "col"), P("col", None), P("row", "col"))
    return jax.shard_map(body, mesh=mesh, in_specs=in_specs, out_specs=out_specs, check_vma=False)
```

```python
import functools
import jax
import jax.numpy as jnp
from jax import lax
from jax.experimental import pallas as pl
from jax.experimental.pallas import tpu as pltpu
from jax.sharding import PartitionSpec as P

highest = lax.Precision.HIGHEST
high = lax.Precision.HIGH
MESH = pl.DeviceIdType.MESH
RANK = 1024
BLK = 128
BASE = 32
SIDE = 4
HALF = RANK // 2


def dot_tn(a, b):
    return lax.dot_general(a, b, (((0,), (0,)), ((), ())), precision=highest, preferred_element_type=jnp.float32)

def dot_nn(a, b):
    return lax.dot_general(a, b, (((1,), (0,)), ((), ())), precision=highest, preferred_element_type=jnp.float32)

def lanes(col):
    return jnp.broadcast_to(col, (8, BLK))

def eliminate(tiles, off, fill):
    lane = lax.broadcasted_iota(jnp.int32, (8, BLK), 1)
    sub = lax.broadcasted_iota(jnp.int32, (8, BLK), 0)
    n = len(tiles)
    done = []
    for g in range(n):
        first = off + 8 * g
        cols = [[lanes(tiles[t][:, first + j:first + j + 1]) for j in range(8)] for t in range(g, n)]
        inside = (lane >= first) & (lane < first + 8)
        tiles[g] = jnp.where(inside, jnp.where(lane - first == sub, 1.0, 0.0), tiles[g])
        for t in range(g + 1, n):
            tiles[t] = jnp.where(inside, 0.0, tiles[t])
        el = [[jnp.broadcast_to(cols[0][j][i:i + 1, :], (8, BLK)) if j >= i else None for j in range(8)] for i in range(8)]
        scale = jnp.zeros((8, BLK), jnp.float32)
        for i in range(8):
            rinv = pl.reciprocal(el[i][i], approx=True)
            rinv = rinv * (2.0 - el[i][i] * rinv)
            scale = jnp.where(sub == i, el[i][i], scale)
            mult = [None] * 8
            for j in range(i + 1, 8):
                mult[j] = el[i][j] * rinv
                for l in range(j, 8):
                    el[j][l] = el[j][l] - mult[j] * el[i][l]
            row = jnp.broadcast_to(tiles[g][i:i + 1, :], (8, BLK)) * rinv
            for t in range(g, n):
                c = cols[t - g][i]
                for j in range(i + 1, 8):
                    cols[t - g][j] = cols[t - g][j] - c * mult[j]
                if t == g:
                    c = jnp.where(sub > i, c, 0.0)
                tiles[t] = tiles[t] - c * row
        done.append(tiles[g] * lax.rsqrt(scale))
        fill()
    full = jnp.concatenate(done, axis=0)
    ln = lax.broadcasted_iota(jnp.int32, full.shape, 1) - off
    rw = lax.broadcasted_iota(jnp.int32, full.shape, 0)
    return jnp.where((ln > rw) & (ln < 8 * n), 0.0, full)

def invert_block(work, at, fill):
    lane = lax.broadcasted_iota(jnp.int32, (BLK, BLK), 1)
    blk = work[pl.ds(at, BLK), pl.ds(at, BLK)]
    parts = []
    for b in range(BLK // BASE):
        lo = b * BASE
        rows = blk[0:BASE, :]
        tiles = [rows[8 * t:8 * t + 8, :] for t in range(BASE // 8)]
        s = eliminate(tiles, lo, fill)
        parts.append(s)
        if lo + BASE < BLK:
            upd = dot_tn(s, s)
            rest = blk[BASE:, :]
            ln = lax.broadcasted_iota(jnp.int32, rest.shape, 1)
            blk = jnp.where((ln >= lo) & (ln < lo + BASE), 0.0, rest) - upd[lo + BASE:, :]
    f = jnp.concatenate(parts, axis=0)
    row = lax.broadcasted_iota(jnp.int32, (BLK, BLK), 0)
    return jnp.where(row >= lane, f, 0.0)


NN = ((1,), (0,))
NT = ((1,), (1,))


def split(x):
    hi = x.astype(jnp.bfloat16)
    return hi, (x - hi.astype(jnp.float32)).astype(jnp.bfloat16)


def dot3(a, b, contract):
    one = functools.partial(
        lax.dot_general, dimension_numbers=(contract, ((), ())), preferred_element_type=jnp.float32
    )
    return one(a[0], b[0]) + (one(a[0], b[1]) + one(a[1], b[0]))

TN = ((0,), (0,))


def inverse_kernel(place_ref, proj_hbm, out_hbm, ortho_hbm, proj_ref, out_ref, ortho_ref, work, hi, lo_part,
                   proj_sem, out_sem, ortho_sem):
    nb = RANK // BLK
    wide = 2 * BLK
    queue = []

    def fill():
        if queue:
            queue.pop(0)()

    def gram(pair, col):
        rows, cols = slice(pair * wide, pair * wide + wide), slice(col * wide, col * wide + wide)
        work[rows, cols] = dot3((hi[:, rows], lo_part[:, rows]), (hi[:, cols], lo_part[:, cols]), TN)

    def right(i, first, last, lo, up):
        at = i * BLK
        left = slice(first * BLK, last * BLK)
        work[at:at + BLK, lo:up] -= dot_tn(work[left, at:at + BLK], work[left, lo:up])

    def left(i, c, last):
        at, lo = i * BLK, c * BLK
        rows = slice(lo, last * BLK)
        work[at:at + BLK, lo:lo + BLK] = -dot3(split(work[rows, at:at + BLK]), split(work[rows, lo:lo + BLK]), TN)

    def ortho(pair):
        cols = slice(pair * wide, pair * wide + wide)
        mine = pl.ds(pl.multiple_of(place_ref[0] * ortho_ref.shape[0], 512), ortho_ref.shape[0])
        deep = pair * wide + wide
        ortho_ref[:, cols] = dot3((hi[mine, :deep], lo_part[mine, :deep]), split(out_ref[cols, :deep]), NT)

    def later(f, *args):
        queue.append(functools.partial(f, *args))

    stores = []

    def store(src, dst, sem):
        copy = pltpu.make_async_copy(src, dst, sem)
        copy.start()
        stores.append(copy)

    chunk = proj_ref.shape[0] // SIDE
    loads = [
        pltpu.make_async_copy(proj_hbm.at[pl.ds(i * chunk, chunk)], proj_ref.at[pl.ds(i * chunk, chunk)], proj_sem.at[i])
        for i in range(SIDE)
    ]
    for copy in loads:
        copy.start()
    for i in range(SIDE):
        loads[i].wait()
        part = slice(i * chunk, i * chunk + chunk)
        hi[part, :], lo_part[part, :] = split(proj_ref[part, :])
    for col in range(RANK // wide):
        gram(0, col)
    for j in range(nb):
        at = j * BLK
        if j % 2 == 0 and j + 2 < nb:
            for col in range(j // 2 + 1, RANK // wide):
                later(gram, j // 2 + 1, col)
        if j and j + 1 < nb:
            for lo in range(at + BLK, RANK, wide):
                later(right, j + 1, 0, j, lo, min(lo + wide, RANK))
            for c in range(j):
                later(left, j + 1, c, j)
        if j and j % 2 == 0:
            later(ortho, j // 2 - 1)
        f = invert_block(work, at, fill)
        while queue:
            fill()
        if at:
            work[at:at + BLK, 0:at] = dot3(split(f), split(work[at:at + BLK, 0:at]), NN)
        if j + 1 < nb:
            work[at:at + BLK, at + BLK:] = dot_nn(f, work[at:at + BLK, at + BLK:])
        work[at:at + BLK, at:at + BLK] = f
        out_ref[at:at + BLK, 0:at + BLK] = work[at:at + BLK, 0:at + BLK]
        if j + 1 == nb:
            store(out_ref.at[pl.ds(at, BLK)], out_hbm.at[pl.ds(at, BLK)], out_sem.at[j])
        if j + 1 < nb:
            out_ref[at:at + BLK, at + BLK:] = jnp.zeros((BLK, RANK - at - BLK), jnp.float32)
            store(out_ref.at[pl.ds(at, BLK)], out_hbm.at[pl.ds(at, BLK)], out_sem.at[j])
            right(j + 1, j, j + 1, at + BLK, RANK)
            nxt = at + BLK
            if at:
                work[nxt:nxt + BLK, 0:at] -= dot3(
                    split(work[at:at + BLK, nxt:nxt + BLK]), split(work[at:at + BLK, 0:at]), TN
                )
            work[nxt:nxt + BLK, at:nxt] = -dot3(split(work[at:at + BLK, nxt:nxt + BLK]), split(f), TN)
    ortho(RANK // wide - 1)
    store(ortho_ref, ortho_hbm, ortho_sem)
    for copy in stores:
        copy.wait()


def inverse_factor(place, projected):
    rows = projected.shape[0]
    hbm = pl.BlockSpec(memory_space=pltpu.HBM)
    flat, square = (rows, RANK), (RANK, RANK)
    sem = pltpu.SemaphoreType.DMA
    return pl.pallas_call(
        inverse_kernel,
        out_shape=[
            jax.ShapeDtypeStruct(square, jnp.float32),
            jax.ShapeDtypeStruct((rows // SIDE, RANK), jnp.float32),
        ],
        in_specs=[pl.BlockSpec(memory_space=pltpu.SMEM), hbm],
        out_specs=[hbm, hbm],
        scratch_shapes=[
            pltpu.VMEM(flat, jnp.float32), pltpu.VMEM(square, jnp.float32),
            pltpu.VMEM((rows // SIDE, RANK), jnp.float32), pltpu.VMEM(square, jnp.float32),
            pltpu.VMEM(flat, jnp.bfloat16), pltpu.VMEM(flat, jnp.bfloat16),
            sem((SIDE,)), sem((RANK // BLK,)), sem(()),
        ],
        compiler_params=pltpu.CompilerParams(vmem_limit_bytes=52 * 2**20),
        cost_estimate=pl.CostEstimate(flops=60 * 10**9, bytes_accessed=18 * 2**20, transcendentals=0),
        name="inverse_factor",
    )(place, projected)


def place():
    col = lax.axis_index("col")
    return lax.axis_index("row"), col // (2 * SIDE), lax.rem(col // 2, SIDE), lax.rem(col, 2)


def ring(at, step):
    return lax.rem(at + step, SIDE)


def device(z, x, y, core):
    return (z, (x * SIDE + y) * 2 + core)


def greet(peers):
    barrier = pltpu.get_barrier_semaphore()
    for peer in peers:
        pl.semaphore_signal(barrier, inc=1, device_id=peer, device_id_type=MESH)
    pl.semaphore_wait(barrier, len(peers))


def remote(src, dst, send, recv, to):
    return pltpu.make_async_remote_copy(
        src_ref=src, dst_ref=dst, send_sem=send, recv_sem=recv, device_id=to, device_id_type=MESH
    )


def gather_kernel(part_ref, turned_ref, hbm_ref, rows_ref, out_ref, paired, total, far, near, sums, slots2, relay, *sems):
    (pair_s, pair_r, far_s, far_r, near_s, near_r, rs2_s, rs2_r, z_s, z_r, in_s, in_r, out_s, out_r,
     fwd_s, fwd_r, hop_s, hop_r, pass_s, pass_r, give_s, give_r, keep) = sems
    z, x, y, core = place()
    lanes_of = (pl.ds(0, HALF), pl.ds(HALF, HALF))
    outer = (x, y)
    inner = (y, x)

    def outer_peer(h, step):
        return device(z, ring(x, step), y, core) if h == 0 else device(z, x, ring(y, step), core)

    def inner_peer(h, step):
        return outer_peer(1 - h, step)

    turn = (1, SIDE - 1)
    twin = device(z, x, y, 1 - core)
    sides = [outer_peer(h, step) for h in range(2) for step in range(1, SIDE)]
    stack = [device(ring(z, step), x, y, core) for step in range(1, SIDE)]
    greet([twin] + sides + stack)
    sent = []

    def push(*args):
        copy = remote(*args)
        copy.start()
        sent.append(copy)
        return copy

    swap = push(part_ref.at[1 - core], paired, pair_s, pair_r, twin)

    share, slab_rows = rows_ref.shape[0], turned_ref.shape[1]
    part = share // 2

    def columns(to, side):
        return turned_ref.at[pl.ds(pl.multiple_of(to * share + side * part, 8), part), :]

    hops = []
    for side in range(2):
        hops.append(
            push(columns(ring(z, 2), side), relay.at[side], hop_s.at[side, 0], hop_r.at[side, 0], stack[turn[side] - 1])
        )

    def landing(slab, side):
        return rows_ref.at[pl.ds(side * part, part), pl.ds(pl.multiple_of(slab * slab_rows, 128), slab_rows)]

    swap.wait_recv()
    total[...] = part_ref[core] + paired[...]
    half_rows = (pl.ds(0, 32), pl.ds(32, 32))
    first, early = {}, {}
    for h in range(2):
        for side in range(2):
            first[h, side] = push(
                total.at[ring(outer[h], 2), half_rows[side], lanes_of[h]], far.at[h, side],
                far_s.at[h, side], far_r.at[h, side], outer_peer(h, turn[side]),
            )
        for side in range(2):
            early[h, side] = push(
                total.at[ring(outer[h], turn[side]), half_rows[1 - side], lanes_of[h]], near.at[h, side, half_rows[1 - side]],
                near_s.at[h, side, 0], near_r.at[h, side, 0], outer_peer(h, turn[side]),
            )
    late = {}
    for h in range(2):
        for side in range(2):
            first[h, side].wait_recv()
            block = ring(outer[h], turn[side])
            total[block, 32 * side:32 * side + 32, h * HALF:(h + 1) * HALF] += far[h, side]
            late[h, side] = push(
                total.at[block, half_rows[side], lanes_of[h]], near.at[h, side, half_rows[side]],
                near_s.at[h, side, 1], near_r.at[h, side, 1], outer_peer(h, turn[side]),
            )
    second = [[None] * 3, [None] * 3]
    for h in range(2):
        for side in range(2):
            early[h, side].wait_recv()
            late[h, side].wait_recv()
        summed = total[outer[h], :, h * HALF:(h + 1) * HALF] + near[h, 0] + near[h, 1]
        sums[h] = summed.reshape(SIDE, 16, HALF)
        for step in (2, 1, 3):
            second[h][step - 1] = push(
                sums.at[h, ring(inner[h], step)], slots2.at[h, step - 1],
                rs2_s.at[h, step - 1], rs2_r.at[h, step - 1], inner_peer(h, step),
            )

    up = [[None] * 3, [None] * 3]
    for h in range(2):
        for copy in second[h]:
            copy.wait_recv()
        done = sums[h, inner[h]] + slots2[h, 0] + slots2[h, 1] + slots2[h, 2]
        out_ref[z, core, outer[h], inner[h], :, h * HALF:(h + 1) * HALF] = done
        own = out_ref.at[z, core, outer[h], inner[h], :, lanes_of[h]]
        for step in (2, 1, 3):
            up[h][step - 1] = push(own, own, z_s.at[h, step - 1], z_r.at[h, step - 1], stack[step - 1])

    rows_ref[:, pl.ds(pl.multiple_of(z * slab_rows, 128), slab_rows)] = turned_ref[
        pl.ds(pl.multiple_of(z * share, 8), share), :
    ]

    def spread(h, at, peer, ref_of, cuts, send, recv, fwd_send, fwd_recv):
        count = len(cuts)
        order = (list(range(count)), list(range(count // 2, count)) + list(range(count // 2)))
        copies, passed = {}, {}
        for k in range(count):
            for side in range(2):
                cut = order[side][k]
                ref = ref_of(cuts[cut], at)
                copies[side, cut] = push(ref, ref, send.at[h, side, cut], recv.at[h, side, cut], peer(h, turn[side]))

        def relay_on(k):
            for side in range(2):
                cut = order[side][k]
                copies[side, cut].wait_recv()
                ref = ref_of(cuts[cut], ring(at, turn[1 - side]))
                passed[cut] = push(ref, ref, fwd_send.at[h, cut], fwd_recv.at[h, cut], peer(h, turn[side]))

        def wait_side(side):
            for k in range(count // 2, count):
                copies[side, order[side][k]].wait_recv()

        def wait_passed():
            for cut in range(count):
                passed[cut].wait_recv()

        return relay_on, wait_side, wait_passed

    back = []
    for h in range(2):
        for copy in up[h]:
            copy.wait_recv()

        def strip(cut, at, h=h):
            return out_ref.at[cut, core, outer[h], at, :, lanes_of[h]]

        back.append(spread(h, inner[h], inner_peer, strip, (pl.ds(0, 2), pl.ds(2, 2)), in_s, in_r, pass_s, pass_r))
    for side in range(2):
        hops[side].wait_recv()
        ref = relay.at[side]
        hops.append(
            push(ref, landing(ring(z, turn[1 - side]), side), hop_s.at[side, 1], hop_r.at[side, 1], stack[turn[side] - 1])
        )
        for half in range(2):
            hops.append(
                push(
                    columns(ring(z, turn[side]), half), landing(z, half),
                    hop_s.at[side, 2 + half], hop_r.at[side, 2 + half], stack[turn[side] - 1],
                )
            )
    for h in range(2):
        back[h][0](0)

    def give(h, group, at):
        ref = out_ref.at[:, core, group, :, :, lanes_of[h]]
        return push(ref, ref, give_s.at[h, at], give_r.at[h, at], twin)

    ahead, got = [], []
    for h in range(2):
        for side in range(2):
            back[h][1](side)
        back[h][2]()

        def block(cut, at, h=h):
            return out_ref.at[cut, core, at, :, :, lanes_of[h]]

        ahead.append(spread(h, outer[h], outer_peer, block, tuple(range(SIDE)), out_s, out_r, fwd_s, fwd_r))
    for h in range(2):
        got.append(give(h, outer[h], 0))
    for k in range(2):
        for h in range(2):
            ahead[h][0](k)
    for h in range(2):
        for side in range(2):
            ahead[h][1](side)
            got.append(give(h, ring(outer[h], turn[1 - side]), 1 + side))
    for h in range(2):
        ahead[h][2]()
        got.append(give(h, ring(outer[h], 2), 3))
    for copy in got + hops[2:]:
        copy.wait_recv()
    store = pltpu.make_async_copy(out_ref, hbm_ref, keep)
    store.start()
    for copy in sent:
        copy.wait_send()
    store.wait()


def turn_kernel(buffer_ref, turned_ref):
    for at in range(0, buffer_ref.shape[1], BLK):
        turned_ref[at:at + BLK, :] = buffer_ref[:, at:at + BLK].T


def turn(buffer):
    vmem = pl.BlockSpec(memory_space=pltpu.VMEM)
    return pl.pallas_call(
        turn_kernel,
        out_shape=jax.ShapeDtypeStruct(buffer.shape[::-1], jnp.float32),
        in_specs=[vmem],
        out_specs=vmem,
        compiler_params=pltpu.CompilerParams(vmem_limit_bytes=12 * 2**20),
        cost_estimate=pl.CostEstimate(flops=10**6, bytes_accessed=7 * 2**20, transcendentals=0),
        name="turn",
    )(buffer)


def gather_projected(part, turned):
    rows = part.shape[0]
    share = turned.shape[0] // SIDE
    sem = pltpu.SemaphoreType.DMA
    pair = lambda *shape: [sem(shape), sem(shape)]
    vmem = pl.BlockSpec(memory_space=pltpu.VMEM)
    full = (SIDE, 2, SIDE, SIDE, 16, RANK)
    out, columns = pl.pallas_call(
        gather_kernel,
        out_shape=[
            jax.ShapeDtypeStruct(full, jnp.float32),
            jax.ShapeDtypeStruct((share, SIDE * rows), jnp.float32),
        ],
        in_specs=[vmem, vmem],
        out_specs=[pl.BlockSpec(memory_space=pltpu.HBM), vmem],
        scratch_shapes=[
            pltpu.VMEM(full, jnp.float32),
            pltpu.VMEM((SIDE, 64, RANK), jnp.float32),
            pltpu.VMEM((SIDE, 64, RANK), jnp.float32),
            pltpu.VMEM((2, 2, 32, HALF), jnp.float32),
            pltpu.VMEM((2, 2, 64, HALF), jnp.float32),
            pltpu.VMEM((2, SIDE, 16, HALF), jnp.float32),
            pltpu.VMEM((2, 3, 16, HALF), jnp.float32),
            pltpu.VMEM((2, share // 2, rows), jnp.float32),
            *pair(), *pair(2, 2), *pair(2, 2, 2), *pair(2, 3), *pair(2, 3), *pair(2, 2, 2), *pair(2, 2, SIDE),
            *pair(2, SIDE), *pair(2, SIDE), *pair(2, 2), *pair(2, SIDE), sem(()),
        ],
        compiler_params=pltpu.CompilerParams(collective_id=0, has_side_effects=True, vmem_limit_bytes=46 * 2**20),
        cost_estimate=pl.CostEstimate(flops=10**6, bytes_accessed=12 * 2**20, transcendentals=0),
        name="gather_projected",
    )(part.reshape(2, SIDE, 64, RANK), turned)
    return out.reshape(SIDE * rows, RANK), columns


def apply_kernel(mixed_hbm, inverse, right_hbm, norm_ref, mixed, stage, right, hi, lo, square, held, slots,
                 in_sem, inv_sem, out_sem, pair_s, pair_r, one_s, one_r, two_s, two_r):
    z, x, y, core = place()
    twin = device(z, x, y, 1 - core)
    along_x = [device(z, ring(x, step), y, core) for step in range(1, SIDE)]
    along_y = [device(z, x, ring(y, step), core) for step in range(1, SIDE)]
    peers = [twin] + along_x + along_y
    barrier = pltpu.get_barrier_semaphore()
    for peer in peers:
        pl.semaphore_signal(barrier, inc=1, device_id=peer, device_id_type=MESH)

    load = pltpu.make_async_copy(inverse, stage, inv_sem)
    load.start()
    rows = mixed_hbm.shape[0] // SIDE
    loads, stores = [], []
    for i in range(SIDE):
        part = pl.ds(i * rows, rows)
        loads.append(pltpu.make_async_copy(mixed_hbm.at[part], mixed.at[part], in_sem.at[i]))
        loads[-1].start()
    load.wait()
    hi[...], lo[...] = split(stage[...])
    for i in range(SIDE):
        at = i * rows
        loads[i].wait()
        left = split(mixed[at:at + rows, :])
        for c in range(0, RANK, 256):
            deep = c + 256
            weight = (hi[c:deep, :deep], lo[c:deep, :deep])
            got = dot3((left[0][:, :deep], left[1][:, :deep]), weight, NT)
            right[at:at + rows, c:deep] = got
            squares = jnp.sum((got * got).reshape(-1, 8, 256), axis=0)
            square[:, c:deep] = squares if i == 0 else square[:, c:deep] + squares
        part = pl.ds(at, rows)
        stores.append(pltpu.make_async_copy(right.at[part], right_hbm.at[part], out_sem.at[i]))
        stores[-1].start()

    held[0] = square[...]
    pl.semaphore_wait(barrier, len(peers))
    swap = remote(held.at[0], slots.at[0], pair_s, pair_r, twin)
    swap.start()
    swap.wait()
    held[1] = held[0] + slots[0]
    for turn, (others, send, recv) in enumerate(((along_x, one_s, one_r), (along_y, two_s, two_r))):
        copies = []
        for step in range(3):
            copy = remote(held.at[1 + turn], slots.at[1 + 3 * turn + step], send.at[step], recv.at[step], others[step])
            copy.start()
            copies.append(copy)
        for copy in copies:
            copy.wait()
        first = 1 + 3 * turn
        held[2 + turn] = held[1 + turn] + slots[first] + slots[first + 1] + slots[first + 2]
    norm_ref[...] = held[3]
    for copy in stores:
        copy.wait()


def apply_inverse(mixed, inverse):
    shape = mixed.shape
    square = (RANK, RANK)
    flat = (8, RANK)
    hbm = pl.BlockSpec(memory_space=pltpu.HBM)
    sem = pltpu.SemaphoreType.DMA
    return pl.pallas_call(
        apply_kernel,
        out_shape=[jax.ShapeDtypeStruct(shape, jnp.float32), jax.ShapeDtypeStruct(flat, jnp.float32)],
        in_specs=[hbm, hbm],
        out_specs=[hbm, pl.BlockSpec(memory_space=pltpu.VMEM)],
        scratch_shapes=[
            pltpu.VMEM(shape, jnp.float32), pltpu.VMEM(square, jnp.float32), pltpu.VMEM(shape, jnp.float32),
            pltpu.VMEM(square, jnp.bfloat16), pltpu.VMEM(square, jnp.bfloat16), pltpu.VMEM(flat, jnp.float32),
            pltpu.VMEM((4,) + flat, jnp.float32), pltpu.VMEM((7,) + flat, jnp.float32),
            sem((SIDE,)), sem(()), sem((SIDE,)), sem(()), sem(()), sem((3,)), sem((3,)), sem((3,)), sem((3,)),
        ],
        compiler_params=pltpu.CompilerParams(collective_id=1, has_side_effects=True, vmem_limit_bytes=58 * 2**20),
        cost_estimate=pl.CostEstimate(flops=8 * 10**9, bytes_accessed=18 * 2**20, transcendentals=0),
        name="apply_inverse",
    )(mixed, inverse)


def dot(a, b, contract, precision):
    return lax.dot_general(a, b, (contract, ((), ())), precision=precision, preferred_element_type=jnp.float32)


def body(momentum, gradient, basis):
    total_cols = basis.shape[0] * lax.axis_size("col")
    buffer = momentum + gradient.astype(jnp.float32)
    place_z = lax.axis_index("row").astype(jnp.int32)
    local_proj = dot(buffer, basis, NN, high)
    projected, columns = gather_projected(local_proj, turn(buffer))
    mixed = dot(columns, projected, NN, high)
    mixed = lax.all_gather(mixed, "row", axis=0, tiled=True)
    inverse, orthonormal = inverse_factor(place_z.reshape(1), projected)
    right_factor, squares = apply_inverse(mixed, inverse)
    squares = jnp.sum(squares, axis=0)
    col_scale = jnp.sqrt(squares / total_cols + 1e-06)
    new_basis = right_factor / col_scale[None, :]
    feedback = dot(orthonormal, right_factor, NT, lax.Precision.DEFAULT)
    new_momentum = buffer - 0.05 * feedback
    update = dot(orthonormal, new_basis, NT, high)
    return (new_momentum, new_basis, update.astype(jnp.bfloat16))


def solution(mesh):
    in_specs = (P("row", "col"), P("row", "col"), P("col", None))
    out_specs = (P("row", "col"), P("col", None), P("row", "col"))
    return jax.shard_map(body, mesh=mesh, in_specs=in_specs, out_specs=out_specs, check_vma=False)
```
